128 devices in a mesh: rows: 32 (over y, x, core), cols: 4 (over z).
Axes of the slice: x: 4, y: 4, z: 4, core: 2. Of those that a mesh axis runs over, the one named last changes fastest.
Arguments:
- descriptors: bfloat16 [196608, 1024], P('rows'), may hold values from -6 to 6
- struct_atoms: int32 [196608], P('rows'), may hold values from 8 to 512
- env_count: int32 [32], P('rows'), may hold values from 1024 to 6144, as said below
- sparse_desc: bfloat16 [2048, 1024], P('cols'), may hold values from -6 to 6
- panel_pick: int32 [256], replicated, may hold values from 0 to 2047, as said below
Outputs:
- kernel_rows: bfloat16 [196608, 2048], P('rows', 'cols')
- panel_r: float32 [256, 256], P('rows')
- cross_gram: float32 [256, 2048], P('rows', 'cols')
The draws below stay inside these ranges and needn't reach their ends.
Inputs may be any that keep to these rules, and one draw needn't show every extreme that they name: Row block r holds its environments in its first env_count[r] slots; the rest of its 6144 slots are empty and their contents are ignored. The counts sum to 65536, and in every draw one row block holds exactly 6144. `panel_pick`: the entries are distinct.
All inputs are finite; a program needn't handle non-finite values.
Results may differ from the reference program's by a relative error of at most 0.013.
Values may be sent and summed in bfloat16 or wider, within the bound.
A program may use at most 128 MiB of HBM per device.

```python
import jax
import jax.numpy as jnp
from jax import lax

DESC = 1024
SPARSE = 2048
PANEL = 256
ENV_DEV = 2048
CAP = 6144
ENVS = 65536
SLOTS = 196608


def draw_env_count(key, part):
    key = jax.random.fold_in(key, 11)
    blocks = ENVS // ENV_DEV
    first_key, second_key = jax.random.split(key)
    busiest = jax.random.randint(first_key, (), 0, blocks)
    shares = jax.random.randint(second_key, (blocks,), 500, 1001)
    positions = jnp.arange(blocks)
    shares = jnp.where(positions == busiest, 0, shares)
    spare_rows = ENVS - CAP - (blocks - 1) * (ENV_DEV // 2)
    extra_rows = spare_rows * shares // jnp.sum(shares)
    leftover = spare_rows - jnp.sum(extra_rows)
    counts = jnp.where(positions == busiest, CAP, ENV_DEV // 2 + extra_rows)
    counts = counts + jnp.where(positions == (busiest + 1) % blocks, leftover, 0)
    return counts.astype(jnp.int32)


def draw_panel_pick(key, part):
    key = jax.random.fold_in(key, 23)
    return jax.random.permutation(key, SPARSE)[:PANEL].astype(jnp.int32)


def touch_ends(values, key, smallest, high):
    extent = values.shape
    place = [jax.random.randint(jax.random.fold_in(key, axis), (), 0, extent[axis]) for axis in range(len(extent))]
    values = values.at[tuple(place)].set(smallest)
    longest = extent.index(max(extent))
    place[longest] = (place[longest] + 1) % extent[longest]
    return values.at[tuple(place)].set(high)


def block_scale(key, extent, shards, least, high):
    gain = 1.0
    for dim, parts in shards:
        steps = jax.random.uniform(jax.random.fold_in(jax.random.fold_in(key, 6), dim), (parts,), jnp.float32, least / len(shards), high / len(shards))
        gain = gain * jnp.repeat(jnp.exp(steps), extent[dim] // parts).reshape((-1,) + (1,) * (len(extent) - 1 - dim))
    return gain


def noise(stream_key, shape, spread, reach, shards=(), held_as=jnp.bfloat16):
    array = jax.random.normal(stream_key, shape, jnp.float32) * spread
    if len(shards) > 0:
        array = block_scale(stream_key, shape, shards, -0.22, 0.18) * array
    return jnp.clip(array, min=-reach, max=reach).astype(held_as)


def setup_inputs(seed: int = 0) -> dict:
    key_of = jax.random.split(jax.random.key(seed), 6)
    descriptors = noise(key_of[0], (SLOTS, DESC), 1.0, 6.0, ((0, 32),))
    struct_atoms = touch_ends(jax.random.randint(key_of[1], (SLOTS,), 8, 513), jax.random.fold_in(key_of[1], 1), 8, 512).astype(jnp.int32)
    env_count = draw_env_count(jax.random.fold_in(key_of[5], 71), 0)
    sparse_desc = noise(key_of[3], (SPARSE, DESC), 1.0, 6.0, ((0, 4),))
    panel_pick = draw_panel_pick(jax.random.fold_in(key_of[5], 71), 0)
    return dict(descriptors=descriptors, struct_atoms=struct_atoms, env_count=env_count, sparse_desc=sparse_desc, panel_pick=panel_pick)


def unit_rows(values):
    wide = values.astype(jnp.float32)
    return (wide * lax.rsqrt(lax.optimization_barrier(jnp.mean(wide * wide, axis=1, keepdims=True)) + 1e-06)).astype(jnp.bfloat16)

def row_weight(atom_counts):
    return (8.0 * lax.rsqrt(atom_counts.astype(jnp.float32))).astype(jnp.bfloat16)

def weighted_kernel(env_units, point_units, weights):
    inner = lax.dot_general(env_units.astype(jnp.float32), point_units.astype(jnp.float32), (((1,), (1,)), ((), ())), preferred_element_type=jnp.float32)
    return weights.astype(jnp.float32)[:, None] * inner * inner / env_units.shape[1]

def reference(descriptors, struct_atoms, env_count, sparse_desc, panel_pick):
    blocks = env_count.shape[0]
    slot_count = descriptors.shape[0] // blocks
    counts = env_count.astype(jnp.int32)
    starts = (jnp.cumsum(counts) - counts).astype(jnp.int32)
    order = jnp.arange(ENVS, dtype=jnp.int32)
    owner = lax.optimization_barrier(jnp.sum((starts[None, 1:] <= order[:, None]).astype(jnp.int32), axis=1)).astype(jnp.int32)
    slot_index = (owner * slot_count + order - starts[owner]).astype(jnp.int32)
    env_units = unit_rows(descriptors[slot_index])
    weights = row_weight(struct_atoms[slot_index])
    point_units = unit_rows(sparse_desc)
    kernel_f = weighted_kernel(env_units, point_units, weights)
    kernel_b = kernel_f.astype(jnp.bfloat16)
    kernel_rows = jnp.zeros((descriptors.shape[0], sparse_desc.shape[0]), jnp.bfloat16).at[slot_index].set(kernel_b)
    panel_f = kernel_f[:, panel_pick]
    panel_b = panel_f.astype(jnp.bfloat16)
    cross_gram = jnp.dot(panel_b.T.astype(jnp.float32), kernel_b.astype(jnp.float32), preferred_element_type=jnp.float32) / ENVS
    factor = jnp.linalg.qr(panel_f / jnp.sqrt(jnp.float32(ENVS)), mode='r')
    panel_r = factor * jnp.sign(jnp.diagonal(factor))[:, None]
    return (kernel_rows, panel_r, cross_gram)
```

```python
import functools

import jax
import jax.numpy as jnp
from jax import lax
from jax.experimental import pallas as pl
from jax.experimental.pallas import tpu as pltpu
from jax.sharding import PartitionSpec as P

MESH = pl.DeviceIdType.MESH
F32 = jnp.float32
BF16 = jnp.bfloat16
TILE = 8
LANES = 128


def signal_group(barrier, n_rows, n_cols, me, group):
    def greet_row(k, carry):
        pl.semaphore_signal(
            barrier, inc=1, device_id=(lax.rem(me + k, n_rows), group), device_id_type=MESH
        )
        return carry

    lax.fori_loop(1, n_rows, greet_row, 0)
    for k in range(1, n_cols):
        pl.semaphore_signal(
            barrier, inc=1, device_id=(me, lax.rem(group + k, n_cols)), device_id_type=MESH
        )
    pl.semaphore_wait(barrier, n_rows - 1 + n_cols - 1)


def unit_rows(wide):
    mean = jnp.sum(wide * wide, axis=1, keepdims=True) * (1.0 / wide.shape[1])
    return wide * lax.rsqrt(mean + 1e-06)


def pick_kernel(
    n_rows, n_cols, pick_ref, sparse_ref, units_ref, out_ref,
    zbuf, gathered, zsend, zrecv, psend, fsend, precv,
):
    me = lax.axis_index("rows")
    group = lax.axis_index("cols")
    chip, core = me // 2, lax.rem(me, 2)
    n_chips = n_rows // 2
    width, depth = sparse_ref.shape
    half = depth // 2
    signal_group(pltpu.get_barrier_semaphore(), n_rows, n_cols, me, group)

    column = lax.broadcasted_iota(jnp.int32, (16, width), 1) + group * width
    row = lax.broadcasted_iota(jnp.int32, (16, width), 0)
    wanted = jnp.zeros((16, width), jnp.int32)
    for i in range(16):
        wanted = jnp.where(row == i, pick_ref[chip * 16 + i], wanted)
    one_hot = jnp.where(wanted == column, 1.0, 0.0).astype(BF16)
    chosen = jnp.dot(one_hot, sparse_ref[...], preferred_element_type=F32)
    chosen = unit_rows(chosen)
    chosen = jnp.where(core == 0, chosen[:, :half], chosen[:, half:]).astype(BF16)
    zbuf[group] = chosen

    def z_copy(k):
        peer = lax.rem(group + k, n_cols)
        return pltpu.make_async_remote_copy(
            src_ref=zbuf.at[group], dst_ref=zbuf.at[group],
            send_sem=zsend.at[k - 1], recv_sem=zrecv.at[k - 1],
            device_id=(me, peer), device_id_type=MESH,
        )

    for k in range(1, n_cols):
        z_copy(k).start()

    def normalise(i, carry):
        at = pl.ds(pl.multiple_of(i * 64, 64), 64)
        units_ref[at, :] = unit_rows(sparse_ref[at, :].astype(F32)).astype(BF16)
        return carry

    lax.fori_loop(0, width // 64, normalise, 0)
    for k in range(1, n_cols):
        z_copy(k).wait()
    total = zbuf[0].astype(F32)
    for k in range(1, n_cols):
        total = total + zbuf[k].astype(F32)

    def piece(which_chip, which_core):
        return gathered.at[
            pl.ds(pl.multiple_of(which_chip * 16, 16), 16),
            pl.ds(pl.multiple_of(which_core * half, half), half),
        ]

    piece(chip, core)[...] = total.astype(BF16)

    def plane_copy(k):
        return pltpu.make_async_remote_copy(
            src_ref=piece(chip, core), dst_ref=piece(chip, core),
            send_sem=psend.at[k], recv_sem=precv.at[core, chip],
            device_id=(lax.rem(chip + k, n_chips) * 2 + core, group), device_id_type=MESH,
        )

    def core_copy(source):
        return pltpu.make_async_remote_copy(
            src_ref=piece(source, core), dst_ref=piece(source, core),
            send_sem=fsend.at[source], recv_sem=precv.at[core, source],
            device_id=(chip * 2 + 1 - core, group), device_id_type=MESH,
        )

    def arrival(source, which_core):
        return pltpu.make_async_remote_copy(
            src_ref=piece(source, which_core), dst_ref=piece(source, which_core),
            send_sem=psend.at[0], recv_sem=precv.at[which_core, source],
            device_id=(me, group), device_id_type=MESH,
        )

    core_copy(chip).start()

    def send(k, carry):
        plane_copy(k).start()
        return carry

    lax.fori_loop(1, n_chips, send, 0)

    def forward(k, carry):
        source = lax.rem(chip + n_chips - k, n_chips)
        arrival(source, core).wait_recv()
        core_copy(source).start()
        return carry

    lax.fori_loop(1, n_chips, forward, 0)

    def finish(k, carry):
        source = lax.rem(chip + n_chips - k, n_chips)
        arrival(source, 1 - core).wait_recv()
        core_copy(source).wait_send()
        return carry

    lax.fori_loop(0, n_chips, finish, 0)

    def sent(k, carry):
        plane_copy(k).wait_send()
        return carry

    lax.fori_loop(1, n_chips, sent, 0)
    out_ref[...] = gathered[...]


def gather_picks(panel_pick, sparse_desc, n_rows, n_cols):
    width, depth = sparse_desc.shape
    panel = panel_pick.shape[0]
    n_chips = n_rows // 2
    return pl.pallas_call(
        functools.partial(pick_kernel, n_rows, n_cols),
        out_shape=(
            jax.ShapeDtypeStruct((width, depth), BF16),
            jax.ShapeDtypeStruct((panel, depth), BF16),
        ),
        in_specs=[
            pl.BlockSpec(memory_space=pltpu.SMEM),
            pl.BlockSpec(memory_space=pltpu.VMEM),
        ],
        out_specs=(pl.BlockSpec(memory_space=pltpu.VMEM),) * 2,
        scratch_shapes=[
            pltpu.VMEM((n_cols, 16, depth // 2), BF16),
            pltpu.VMEM((panel, depth), BF16),
            pltpu.SemaphoreType.DMA((n_cols - 1,)),
            pltpu.SemaphoreType.DMA((n_cols - 1,)),
            pltpu.SemaphoreType.DMA((n_chips,)),
            pltpu.SemaphoreType.DMA((n_chips,)),
            pltpu.SemaphoreType.DMA((2, n_chips)),
        ],
        compiler_params=pltpu.CompilerParams(
            collective_id=0, has_side_effects=True, vmem_limit_bytes=16 * 2**20
        ),
        name="gather_picks",
    )(panel_pick, sparse_desc)


def env_kernel(
    env_total, count_ref, x_ref, atoms_ref, units_ref, picks_ref,
    rows_ref, gram_ref, cross_ref, points, acc,
):
    step = pl.program_id(0)
    rows, depth = x_ref.shape
    width, panel = units_ref.shape[0], picks_ref.shape[0]
    count = count_ref[0]

    @pl.when(step == 0)
    def _():
        points[:width, :] = units_ref[...]
        points[width:, :] = picks_ref[...]
        acc[...] = jnp.zeros_like(acc)

    @pl.when(step * rows >= count)
    def _():
        rows_ref[...] = jnp.zeros_like(rows_ref)

    @pl.when(step * rows < count)
    def _():
        x = x_ref[...]
        wide = x.astype(F32)
        mean = jnp.sum(wide * wide, axis=1, keepdims=True) * (1.0 / depth)
        atoms = atoms_ref[0].astype(F32)
        weight = (8.0 * lax.rsqrt(atoms)).astype(BF16).astype(F32)
        lines = atoms.shape[0]
        slot = (
            step * rows
            + lax.broadcasted_iota(jnp.int32, atoms.shape, 0) * LANES
            + lax.broadcasted_iota(jnp.int32, atoms.shape, 1)
        )
        scale = jnp.where(slot < count, jnp.sqrt(weight * (1.0 / depth)), 0.0)
        pad = TILE - lines
        if pad > 0:
            scale = jnp.concatenate([scale, jnp.zeros((pad, LANES), F32)], axis=0)
        columns = scale.T
        scale = jnp.concatenate([columns[:, i : i + 1] for i in range(lines)], axis=0)
        factor = scale * lax.rsqrt(mean + 1e-06)
        inner = lax.dot_general(
            x, points[...], (((1,), (1,)), ((), ())), preferred_element_type=F32
        )
        inner = inner * factor
        kernel = inner * inner
        high = kernel.astype(BF16)
        rows_ref[...] = high[:, :width]
        picked = high[:, width:]
        low = (kernel[:, width:] - picked.astype(F32)).astype(BF16)
        acc[...] += lax.dot_general(
            picked,
            jnp.concatenate([high, low], axis=1),
            (((0,), (0,)), ((), ())),
            preferred_element_type=F32,
        )

    @pl.when(step == pl.num_programs(0) - 1)
    def _():
        scaled = 1.0 / env_total
        mixed = acc[:, width + panel :]
        gram_ref[...] = (acc[:, width : width + panel] + mixed + mixed.T) * scaled
        half = width // 2
        for r in range(panel // TILE):
            part = acc[r * TILE : (r + 1) * TILE, :width] * scaled
            cross_ref[r] = jnp.concatenate([part[:, :half], part[:, half:]], axis=0).astype(BF16)


def env_pass(env_count, descriptors, struct_atoms, units, picks, env_total, block):
    slots, depth = descriptors.shape
    width, panel = units.shape[0], picks.shape[0]
    steps = slots // block
    lines = block // LANES
    return pl.pallas_call(
        functools.partial(env_kernel, env_total),
        grid=(steps,),
        out_shape=(
            jax.ShapeDtypeStruct((slots, width), BF16),
            jax.ShapeDtypeStruct((panel, panel), F32),
            jax.ShapeDtypeStruct((panel // TILE, 2 * TILE, width // 2), BF16),
        ),
        in_specs=[
            pl.BlockSpec(memory_space=pltpu.SMEM),
            pl.BlockSpec((block, depth), lambda i: (i, 0)),
            pl.BlockSpec((1, lines, LANES), lambda i: (i, 0, 0)),
            pl.BlockSpec((width, depth), lambda i: (0, 0)),
            pl.BlockSpec((panel, depth), lambda i: (0, 0)),
        ],
        out_specs=(
            pl.BlockSpec((block, width), lambda i: (i, 0)),
            pl.BlockSpec((panel, panel), lambda i: (0, 0)),
            pl.BlockSpec((panel // TILE, 2 * TILE, width // 2), lambda i: (0, 0, 0)),
        ),
        scratch_shapes=[
            pltpu.VMEM((width + panel, depth), BF16),
            pltpu.VMEM((panel, width + 2 * panel), F32),
        ],
        compiler_params=pltpu.CompilerParams(vmem_limit_bytes=40 * 2**20),
        name="env_pass",
    )(env_count, descriptors, struct_atoms.reshape(steps, lines, LANES), units, picks)


def reduce_kernel(
    n_rows, n_cols, gram_ref, cross_ref, whole_ref, sum_ref,
    gbuf, cbuf, gathered, gsend, grecv, csend, crecv, psend, precv,
):
    me = lax.axis_index("rows")
    group = lax.axis_index("cols")
    half = cross_ref.shape[2]
    signal_group(pltpu.get_barrier_semaphore(), n_rows, 1, me, group)

    def lines(r):
        return pl.ds(pl.multiple_of(r * TILE, TILE), TILE)

    def gram_copy(k):
        peer = lax.rem(me + k, n_rows)
        return pltpu.make_async_remote_copy(
            src_ref=gram_ref.at[lines(peer), :], dst_ref=gbuf.at[me],
            send_sem=gsend.at[k], recv_sem=grecv.at[me],
            device_id=(peer, group), device_id_type=MESH,
        )

    def cross_copy(k):
        peer = lax.rem(me + k, n_rows)
        return pltpu.make_async_remote_copy(
            src_ref=cross_ref.at[peer], dst_ref=cbuf.at[me],
            send_sem=csend.at[k], recv_sem=crecv.at[me],
            device_id=(peer, group), device_id_type=MESH,
        )

    def whole_copy(k):
        peer = lax.rem(me + k, n_rows)
        return pltpu.make_async_remote_copy(
            src_ref=gathered.at[lines(me), :], dst_ref=gathered.at[lines(me), :],
            send_sem=psend.at[k], recv_sem=precv.at[me],
            device_id=(peer, group), device_id_type=MESH,
        )

    def each(body):
        def run(k, carry):
            body(k)
            return carry

        lax.fori_loop(1, n_rows, run, 0)

    each(lambda k: gram_copy(k).start())
    each(lambda k: cross_copy(k).start())
    gbuf[me] = gram_ref[lines(me), :]
    cbuf[me] = cross_ref[me]

    def got_gram(k):
        source = lax.rem(me + n_rows - k, n_rows)
        pltpu.make_async_remote_copy(
            src_ref=gbuf.at[source], dst_ref=gbuf.at[source],
            send_sem=gsend.at[k], recv_sem=grecv.at[source],
            device_id=(me, group), device_id_type=MESH,
        ).wait_recv()

    each(got_gram)
    total = gbuf[0]
    for r in range(1, n_rows):
        total = total + gbuf[r]
    gathered[lines(me), :] = total
    each(lambda k: whole_copy(k).start())

    def got_cross(k):
        source = lax.rem(me + n_rows - k, n_rows)
        pltpu.make_async_remote_copy(
            src_ref=cbuf.at[source], dst_ref=cbuf.at[source],
            send_sem=csend.at[k], recv_sem=crecv.at[source],
            device_id=(me, group), device_id_type=MESH,
        ).wait_recv()

    each(got_cross)
    total = cbuf[0].astype(F32)
    for r in range(1, n_rows):
        total = total + cbuf[r].astype(F32)
    sum_ref[:, :half] = total[:TILE]
    sum_ref[:, half:] = total[TILE:]

    def got_whole(k):
        source = lax.rem(me + n_rows - k, n_rows)
        pltpu.make_async_remote_copy(
            src_ref=gathered.at[lines(source), :], dst_ref=gathered.at[lines(source), :],
            send_sem=psend.at[k], recv_sem=precv.at[source],
            device_id=(me, group), device_id_type=MESH,
        ).wait_recv()

    each(got_whole)

    def all_sent(k):
        gram_copy(k).wait_send()
        cross_copy(k).wait_send()
        whole_copy(k).wait_send()

    each(all_sent)
    whole_ref[...] = gathered[...]


def reduce_rows(gram, cross, n_rows, n_cols):
    panel = gram.shape[0]
    half = cross.shape[2]
    sems = pltpu.SemaphoreType.DMA((n_rows,))
    return pl.pallas_call(
        functools.partial(reduce_kernel, n_rows, n_cols),
        out_shape=(
            jax.ShapeDtypeStruct((panel, panel), F32),
            jax.ShapeDtypeStruct((TILE, 2 * half), F32),
        ),
        in_specs=[pl.BlockSpec(memory_space=pltpu.VMEM)] * 2,
        out_specs=(pl.BlockSpec(memory_space=pltpu.VMEM),) * 2,
        scratch_shapes=[
            pltpu.VMEM((n_rows, TILE, panel), F32),
            pltpu.VMEM((n_rows, 2 * TILE, half), BF16),
            pltpu.VMEM((panel, panel), F32),
        ]
        + [sems] * 6,
        compiler_params=pltpu.CompilerParams(
            collective_id=1, has_side_effects=True, vmem_limit_bytes=16 * 2**20
        ),
        name="reduce_rows",
    )(gram, cross)


def wide_of(tile, lane):
    return jnp.broadcast_to(tile[:, lane : lane + 1], (TILE, LANES))


def tall_of(tile, line):
    return jnp.broadcast_to(tile[line : line + 1, :], (TILE, LANES))


def factor_band(tiles):
    groups, halves = len(tiles), len(tiles[0])
    line = lax.broadcasted_iota(jnp.int32, (TILE, LANES), 0)
    out = []
    for t in range(groups):
        base = t * TILE
        cols = {g: [wide_of(tiles[g][0], base + k) for k in range(TILE)] for g in range(t, groups)}
        low = {(i, k): tall_of(cols[t][k], i) for k in range(TILE) for i in range(k, TILE)}
        inv = []
        for k in range(TILE):
            inv.append(lax.rsqrt(low[k, k]))
            for i in range(k + 1, TILE):
                low[i, k] = low[i, k] * inv[k]
            for m in range(k + 1, TILE):
                for i in range(m, TILE):
                    low[i, m] = low[i, m] - low[i, k] * low[m, k]
        band = []
        for h in range(halves):
            lines = []
            for k in range(TILE):
                value = tall_of(tiles[t][h], k)
                for m in range(k):
                    value = value - low[k, m] * lines[m]
                lines.append(value * inv[k])
            band.append(lines)
        merged = []
        for h in range(halves):
            value = band[h][0]
            for k in range(1, TILE):
                value = jnp.where(line == k, band[h][k], value)
            merged.append(value)
        out.append(merged)
        for g in range(t + 1, groups):
            left = []
            for k in range(TILE):
                value = cols[g][k]
                for m in range(k):
                    value = value - left[m] * low[k, m]
                left.append(value * inv[k])
            for h in range(halves):
                value = tiles[g][h]
                for k in range(TILE):
                    value = value - left[k] * band[h][k]
                tiles[g][h] = value
    return out


def factor_kernel(gram_ref, out_ref, work):
    size = gram_ref.shape[0]
    bands = size // LANES
    groups = LANES // TILE
    work[...] = gram_ref[...]
    line = lax.broadcasted_iota(jnp.int32, (TILE, LANES), 0)
    lane = lax.broadcasted_iota(jnp.int32, (TILE, LANES), 1)
    for b in range(bands):
        tiles = [
            [
                work[b * LANES + g * TILE : b * LANES + (g + 1) * TILE, h * LANES : (h + 1) * LANES]
                for h in range(b, bands)
            ]
            for g in range(groups)
        ]
        factor = factor_band(tiles)
        for g in range(groups):
            first = b * LANES + g * TILE
            for h in range(bands):
                if h < b:
                    value = jnp.zeros((TILE, LANES), F32)
                else:
                    value = factor[g][h - b]
                    if h == b:
                        value = jnp.where(lane >= line + g * TILE, value, 0.0)
                work[first : first + TILE, h * LANES : (h + 1) * LANES] = value
        if b + 1 < bands:
            right = work[b * LANES : (b + 1) * LANES, (b + 1) * LANES :]
            work[(b + 1) * LANES :, (b + 1) * LANES :] -= lax.dot_general(
                right, right, (((0,), (0,)), ((), ())),
                precision=lax.Precision.HIGHEST, preferred_element_type=F32,
            )
    if out_ref.shape == work.shape:
        out_ref[...] = work[...]
    else:
        me = lax.axis_index("rows")
        out_ref[...] = work[pl.ds(pl.multiple_of(me * TILE, TILE), TILE), :]


def triangular(gram, full=False):
    size = gram.shape[0]
    return pl.pallas_call(
        factor_kernel,
        out_shape=jax.ShapeDtypeStruct((size if full else TILE, size), F32),
        in_specs=[pl.BlockSpec(memory_space=pltpu.VMEM)],
        out_specs=pl.BlockSpec(memory_space=pltpu.VMEM),
        scratch_shapes=[pltpu.VMEM((size, size), F32)],
        compiler_params=pltpu.CompilerParams(vmem_limit_bytes=16 * 2**20),
        name="triangular",
    )(gram)


def local(descriptors, struct_atoms, env_count, sparse_desc, panel_pick):
    n_rows, n_cols = lax.axis_size("rows"), lax.axis_size("cols")
    slots = descriptors.shape[0]
    env_total = slots // 3 * n_rows
    units, picks = gather_picks(panel_pick, sparse_desc, n_rows, n_cols)
    kernel_rows, gram, cross = env_pass(
        env_count, descriptors, struct_atoms, units, picks, env_total, 512
    )
    whole, cross_gram = reduce_rows(gram, cross, n_rows, n_cols)
    return kernel_rows, triangular(whole), cross_gram


def solution(mesh):
    return jax.shard_map(
        local,
        mesh=mesh,
        in_specs=(P("rows", None), P("rows"), P("rows"), P("cols", None), P()),
        out_specs=(P("rows", "cols"), P("rows", None), P("rows", "cols")),
        check_vma=False,
    )
```

```python
import functools

import jax
import jax.numpy as jnp
from jax import lax
from jax.experimental import pallas as pl
from jax.experimental.pallas import tpu as pltpu
from jax.sharding import PartitionSpec as P

MESH = pl.DeviceIdType.MESH
F32 = jnp.float32
BF16 = jnp.bfloat16
TILE = 8
LANES = 128
MIB = 2**20


def wrap(value, size):
    return jnp.where(value >= size, value - size, value)


def unit_rows(wide):
    mean = jnp.sum(wide * wide, axis=1, keepdims=True) * (1.0 / wide.shape[1])
    return wide * lax.rsqrt(mean + 1e-06)


def each(first, last, body):
    def run(k, carry):
        body(k)
        return carry

    lax.fori_loop(first, last, run, 0)


def gram_kernel(
    n_rows, n_cols, env_total, block,
    pick_ref, count_ref, atoms_ref, sparse_ref, x_ref,
    rows_ref, whole_ref, sum_ref,
    xbuf, kbuf, factor, units, gathered, zbuf, gram, gbuf, total_gram, cross, cbuf,
    picks, count, xsem, osem, isem, zsend, zrecv, psend, fsend, precv, gsend, csend, wsend, rsem,
):
    me = lax.axis_index("rows")
    group = lax.axis_index("cols")
    chip, core = me // 2, lax.rem(me, 2)
    n_chips = n_rows // 2
    slots, depth = xbuf.shape
    width, panel = units.shape[0], gathered.shape[0]
    half, short = depth // 2, width // 2

    def rows_of(i, size):
        return pl.ds(pl.multiple_of(i * size, size), size)

    load_units = pltpu.make_async_copy(sparse_ref, units, isem.at[0])
    load_picks = pltpu.make_async_copy(pick_ref, picks, isem.at[1])
    load_count = pltpu.make_async_copy(count_ref, count, isem.at[2])
    load_units.start()
    load_picks.start()
    load_count.start()
    loads = [
        pltpu.make_async_copy(
            x_ref.at[pl.ds(i * block, block), :], xbuf.at[pl.ds(i * block, block), :], xsem.at[i]
        )
        for i in range(slots // block)
    ]
    for copy in loads:
        copy.start()

    barrier = pltpu.get_barrier_semaphore()
    each(1, n_rows, lambda k: pl.semaphore_signal(
        barrier, inc=1, device_id=(wrap(me + k, n_rows), group), device_id_type=MESH))
    for k in range(1, n_cols):
        pl.semaphore_signal(
            barrier, inc=1, device_id=(me, wrap(group + k, n_cols)), device_id_type=MESH
        )

    load_units.wait()

    load_picks.wait()
    column = lax.broadcasted_iota(jnp.int32, (16, width), 1) + group * width
    row = lax.broadcasted_iota(jnp.int32, (16, width), 0)
    wanted = jnp.zeros((16, width), jnp.int32)
    for i in range(16):
        wanted = jnp.where(row == i, picks[chip * 16 + i], wanted)
    one_hot = jnp.where(wanted == column, 1.0, 0.0).astype(BF16)
    chosen = unit_rows(jnp.dot(one_hot, units[...], preferred_element_type=F32))
    zbuf[group] = jnp.where(core == 0, chosen[:, :half], chosen[:, half:]).astype(BF16)

    def z_copy(k):
        return pltpu.make_async_remote_copy(
            src_ref=zbuf.at[group], dst_ref=zbuf.at[group],
            send_sem=zsend.at[k - 1], recv_sem=zrecv.at[k - 1],
            device_id=(me, wrap(group + k, n_cols)), device_id_type=MESH,
        )

    pl.semaphore_wait(barrier, n_rows - 1 + n_cols - 1)
    for k in range(1, n_cols):
        z_copy(k).start()

    def normalise(i):
        at = rows_of(i, 64)
        units[at, :] = unit_rows(units[at, :].astype(F32)).astype(BF16)

    each(0, width // 64, normalise)
    load_count.wait()
    lines = atoms_ref.shape[0]
    weight = (8.0 * lax.rsqrt(atoms_ref[...].astype(F32))).astype(BF16).astype(F32)
    slot = (
        lax.broadcasted_iota(jnp.int32, atoms_ref.shape, 0) * LANES
        + lax.broadcasted_iota(jnp.int32, atoms_ref.shape, 1)
    )
    columns = jnp.where(slot < count[0], jnp.sqrt(weight * (1.0 / depth)), 0.0).T
    for i in range(lines):
        factor[i * LANES : (i + 1) * LANES, :] = columns[:, i : i + 1]

    def save(i):
        return pltpu.make_async_copy(
            kbuf.at[pl.ds(i * block, block), pl.ds(0, width)],
            rows_ref.at[pl.ds(i * block, block), :],
            osem.at[i],
        )

    def own_points(i):
        at = slice(i * block, (i + 1) * block)
        loads[i].wait()
        x = xbuf[at, :]
        wide = x.astype(F32)
        mean = jnp.sum(wide * wide, axis=1, keepdims=True) * (1.0 / depth)
        scale = factor[at, :] * lax.rsqrt(mean + 1e-06)
        factor[at, :] = scale
        inner = lax.dot_general(
            x, units[...], (((1,), (1,)), ((), ())), preferred_element_type=F32
        ) * scale
        kbuf[at, :width] = (inner * inner).astype(BF16)
        save(i).start()

    def panel_points(i):
        at = slice(i * block, (i + 1) * block)
        inner = lax.dot_general(
            xbuf[at, :], gathered[...], (((1,), (1,)), ((), ())), preferred_element_type=F32
        ) * factor[at, :]
        kbuf[at, width:] = (inner * inner).astype(BF16)

    own_points(0)

    for k in range(1, n_cols):
        z_copy(k).wait()
    total = zbuf[0].astype(F32)
    for k in range(1, n_cols):
        total = total + zbuf[k].astype(F32)

    def piece(which_chip, which_core):
        return gathered.at[rows_of(which_chip, 16), rows_of(which_core, half)]

    piece(chip, core)[...] = total.astype(BF16)

    def plane_copy(k):
        return pltpu.make_async_remote_copy(
            src_ref=piece(chip, core), dst_ref=piece(chip, core),
            send_sem=psend.at[k], recv_sem=precv.at[core, chip],
            device_id=(wrap(chip + k, n_chips) * 2 + core, group), device_id_type=MESH,
        )

    def core_copy(source):
        return pltpu.make_async_remote_copy(
            src_ref=piece(source, core), dst_ref=piece(source, core),
            send_sem=fsend.at[source], recv_sem=precv.at[core, source],
            device_id=(chip * 2 + 1 - core, group), device_id_type=MESH,
        )

    def arrival(source, which_core):
        return pltpu.make_async_copy(
            piece(source, which_core), piece(source, which_core), precv.at[which_core, source]
        )

    each(1, n_chips, lambda k: plane_copy(k).start())
    core_copy(chip).start()
    for i in range(1, slots // block):
        own_points(i)

    def forward(k):
        source = wrap(chip + n_chips - k, n_chips)
        arrival(source, core).wait()
        core_copy(source).start()

    each(1, n_chips, forward)

    def finish(k):
        source = wrap(chip + n_chips - k, n_chips)
        arrival(source, 1 - core).wait()

    each(0, n_chips, finish)
    for i in range(slots // block):
        panel_points(i)

    def transposed_product(right):
        return lax.dot_general(
            kbuf[:, width:], right, (((0,), (0,)), ((), ())), preferred_element_type=F32
        ) * (1.0 / env_total)

    gram[...] = transposed_product(kbuf[:, width:])

    def gram_copy(k):
        peer = wrap(me + k, n_rows)
        return pltpu.make_async_remote_copy(
            src_ref=gram.at[rows_of(peer, TILE), :], dst_ref=gbuf.at[k - 1],
            send_sem=gsend.at[k], recv_sem=rsem.at[0],
            device_id=(peer, group), device_id_type=MESH,
        )

    def cross_copy(k):
        peer = wrap(me + k, n_rows)
        return pltpu.make_async_remote_copy(
            src_ref=cross.at[peer], dst_ref=cbuf.at[k - 1],
            send_sem=csend.at[k], recv_sem=rsem.at[1],
            device_id=(peer, group), device_id_type=MESH,
        )

    def whole_copy(k):
        return pltpu.make_async_remote_copy(
            src_ref=total_gram.at[rows_of(me, TILE), :],
            dst_ref=total_gram.at[rows_of(me, TILE), :],
            send_sem=wsend.at[k], recv_sem=rsem.at[2],
            device_id=(wrap(me + k, n_rows), group), device_id_type=MESH,
        )

    each(1, n_rows, lambda k: gram_copy(k).start())
    product = transposed_product(kbuf[:, :width])
    for r in range(panel // TILE):
        part = product[r * TILE : (r + 1) * TILE, :]
        cross[r] = jnp.concatenate([part[:, :short], part[:, short:]], axis=0).astype(BF16)
    each(1, n_rows, lambda k: cross_copy(k).start())
    pltpu.make_async_copy(gbuf, gbuf, rsem.at[0]).wait()
    total = gram[rows_of(me, TILE), :]
    for r in range(n_rows - 1):
        total = total + gbuf[r]
    total_gram[rows_of(me, TILE), :] = total
    each(1, n_rows, lambda k: whole_copy(k).start())
    pltpu.make_async_copy(cbuf, cbuf, rsem.at[1]).wait()
    total = cross[me].astype(F32)
    for r in range(n_rows - 1):
        total = total + cbuf[r].astype(F32)
    sum_ref[:, :short] = total[:TILE]
    sum_ref[:, short:] = total[TILE:]
    arrived = total_gram.at[pl.ds(0, panel - TILE), :]
    pltpu.make_async_copy(arrived, arrived, rsem.at[2]).wait()
    whole_ref[...] = total_gram[...]

    def all_sent(k):
        gram_copy(k).wait_send()
        cross_copy(k).wait_send()
        whole_copy(k).wait_send()

    each(1, n_rows, all_sent)
    each(1, n_chips, lambda k: plane_copy(k).wait_send())
    each(0, n_chips, lambda k: core_copy(k).wait_send())
    for i in range(slots // block):
        save(i).wait()


def gram_pass(panel_pick, env_count, struct_atoms, sparse_desc, descriptors, n_rows, n_cols, block):
    slots, depth = descriptors.shape
    width, panel = sparse_desc.shape[0], panel_pick.shape[0]
    n_chips = n_rows // 2
    short = width // 2
    hbm = pl.BlockSpec(memory_space=pl.ANY)
    vmem = pl.BlockSpec(memory_space=pltpu.VMEM)
    dma = pltpu.SemaphoreType.DMA
    return pl.pallas_call(
        functools.partial(gram_kernel, n_rows, n_cols, slots // 3 * n_rows, block),
        out_shape=(
            jax.ShapeDtypeStruct((slots, width), BF16),
            jax.ShapeDtypeStruct((panel, panel), F32),
            jax.ShapeDtypeStruct((TILE, width), F32),
        ),
        in_specs=[hbm, hbm, vmem, hbm, hbm],
        out_specs=(hbm, vmem, vmem),
        scratch_shapes=[
            pltpu.VMEM((slots, depth), BF16),
            pltpu.VMEM((slots, width + panel), BF16),
            pltpu.VMEM((slots, 1), F32),
            pltpu.VMEM((width, depth), BF16),
            pltpu.VMEM((panel, depth), BF16),
            pltpu.VMEM((n_cols, 16, depth // 2), BF16),
            pltpu.VMEM((panel, panel), F32),
            pltpu.VMEM((n_rows - 1, TILE, panel), F32),
            pltpu.VMEM((panel, panel), F32),
            pltpu.VMEM((n_rows, 2 * TILE, short), BF16),
            pltpu.VMEM((n_rows - 1, 2 * TILE, short), BF16),
            pltpu.SMEM((panel,), jnp.int32),
            pltpu.SMEM((1,), jnp.int32),
            dma((slots // block,)),
            dma((slots // block,)),
            dma((3,)),
            dma((n_cols - 1,)),
            dma((n_cols - 1,)),
            dma((n_chips,)),
            dma((n_chips,)),
            dma((2, n_chips)),
            dma((n_rows,)),
            dma((n_rows,)),
            dma((n_rows,)),
            dma((3,)),
        ],
        compiler_params=pltpu.CompilerParams(
            collective_id=0, has_side_effects=True, vmem_limit_bytes=56 * MIB
        ),
        name="gram_pass",
    )(panel_pick, env_count, struct_atoms.reshape(slots // LANES, LANES), sparse_desc, descriptors)


def wide_of(tile, lane):
    return jnp.broadcast_to(tile[:, lane : lane + 1], (TILE, LANES))


def tall_of(tile, line):
    return jnp.broadcast_to(tile[line : line + 1, :], (TILE, LANES))


def factor_band(tiles):
    groups, halves = len(tiles), len(tiles[0])
    line = lax.broadcasted_iota(jnp.int32, (TILE, LANES), 0)
    out = []
    for t in range(groups):
        base = t * TILE
        cols = {g: [wide_of(tiles[g][0], base + k) for k in range(TILE)] for g in range(t, groups)}
        low = {(i, k): tall_of(cols[t][k], i) for k in range(TILE) for i in range(k, TILE)}
        inv = []
        for k in range(TILE):
            inv.append(lax.rsqrt(low[k, k]))
            for i in range(k + 1, TILE):
                low[i, k] = low[i, k] * inv[k]
            for m in range(k + 1, TILE):
                for i in range(m, TILE):
                    low[i, m] = low[i, m] - low[i, k] * low[m, k]
        band = []
        for h in range(halves):
            lines = []
            for k in range(TILE):
                value = tall_of(tiles[t][h], k)
                for m in range(k):
                    value = value - low[k, m] * lines[m]
                lines.append(value * inv[k])
            band.append(lines)
        merged = []
        for h in range(halves):
            value = band[h][0]
            for k in range(1, TILE):
                value = jnp.where(line == k, band[h][k], value)
            merged.append(value)
        out.append(merged)
        for g in range(t + 1, groups):
            left = []
            for k in range(TILE):
                value = cols[g][k]
                for m in range(k):
                    value = value - left[m] * low[k, m]
                left.append(value * inv[k])
            for h in range(halves):
                value = tiles[g][h]
                for k in range(TILE):
                    value = value - left[k] * band[h][k]
                tiles[g][h] = value
    return out


def factor_kernel(
    gram_ref, rows_ref, sum_ref, out_ref, kernel_ref, cross_ref, work, passing, sums, isem, osem
):
    size = gram_ref.shape[0]
    parts = osem.shape[0] - 1
    part = rows_ref.shape[0] // parts
    chunks = [pl.ds(i * part, part) for i in range(parts)]
    load = pltpu.make_async_copy(gram_ref, work, isem.at[parts])
    loads = [
        pltpu.make_async_copy(rows_ref.at[c, :], passing.at[c, :], isem.at[i])
        for i, c in enumerate(chunks)
    ]
    loads.append(pltpu.make_async_copy(sum_ref, sums, isem.at[parts + 1]))
    saves = [
        pltpu.make_async_copy(passing.at[c, :], kernel_ref.at[c, :], osem.at[i])
        for i, c in enumerate(chunks)
    ]
    saves.append(pltpu.make_async_copy(sums, cross_ref, osem.at[parts]))
    load.start()
    for copy in loads:
        copy.start()
    load.wait()
    bands = size // LANES
    groups = LANES // TILE
    line = lax.broadcasted_iota(jnp.int32, (TILE, LANES), 0)
    lane = lax.broadcasted_iota(jnp.int32, (TILE, LANES), 1)
    for b in range(bands):
        tiles = [
            [
                work[b * LANES + g * TILE : b * LANES + (g + 1) * TILE, h * LANES : (h + 1) * LANES]
                for h in range(b, bands)
            ]
            for g in range(groups)
        ]
        factor = factor_band(tiles)
        for g in range(groups):
            first = b * LANES + g * TILE
            for h in range(bands):
                if h < b:
                    value = jnp.zeros((TILE, LANES), F32)
                else:
                    value = factor[g][h - b]
                    if h == b:
                        value = jnp.where(lane >= line + g * TILE, value, 0.0)
                work[first : first + TILE, h * LANES : (h + 1) * LANES] = value
        if b == 0:
            for copy, then in zip(loads, saves, strict=True):
                copy.wait()
                then.start()
        if b + 1 < bands:
            right = work[b * LANES : (b + 1) * LANES, (b + 1) * LANES :]
            work[(b + 1) * LANES :, (b + 1) * LANES :] -= lax.dot_general(
                right, right, (((0,), (0,)), ((), ())),
                precision=lax.Precision.HIGHEST, preferred_element_type=F32,
            )
    me = lax.axis_index("rows")
    out_ref[...] = work[pl.ds(pl.multiple_of(me * TILE, TILE), TILE), :]
    for copy in saves:
        copy.wait()


def factor_pass(gram, kernel_rows, cross_sum):
    size = gram.shape[0]
    hbm = pl.BlockSpec(memory_space=pl.ANY)
    vmem = pl.BlockSpec(memory_space=pltpu.VMEM)
    return pl.pallas_call(
        factor_kernel,
        out_shape=(
            jax.ShapeDtypeStruct((TILE, size), F32),
            jax.ShapeDtypeStruct(kernel_rows.shape, BF16),
            jax.ShapeDtypeStruct(cross_sum.shape, F32),
        ),
        in_specs=[hbm, hbm, hbm],
        out_specs=(vmem, hbm, hbm),
        scratch_shapes=[
            pltpu.VMEM((size, size), F32),
            pltpu.VMEM(kernel_rows.shape, BF16),
            pltpu.VMEM(cross_sum.shape, F32),
            pltpu.SemaphoreType.DMA((8,)),
            pltpu.SemaphoreType.DMA((7,)),
        ],
        compiler_params=pltpu.CompilerParams(vmem_limit_bytes=60 * MIB),
        name="factor_pass",
    )(gram, kernel_rows, cross_sum)


def local(descriptors, struct_atoms, env_count, sparse_desc, panel_pick):
    n_rows, n_cols = lax.axis_size("rows"), lax.axis_size("cols")
    kernel_rows, gram, cross_sum = gram_pass(
        panel_pick, env_count, struct_atoms, sparse_desc, descriptors, n_rows, n_cols, 2048
    )
    factor_rows, kernel_rows, cross_gram = factor_pass(gram, kernel_rows, cross_sum)
    return kernel_rows, factor_rows, cross_gram


def solution(mesh):
    return jax.shard_map(
        local,
        mesh=mesh,
        in_specs=(P("rows", None), P("rows"), P("rows"), P("cols", None), P()),
        out_specs=(P("rows", "cols"), P("rows", None), P("rows", "cols")),
        check_vma=False,
    )
```

```python
import functools

import jax
import jax.numpy as jnp
from jax import lax
from jax.experimental import pallas as pl
from jax.experimental.pallas import tpu as pltpu
from jax.sharding import PartitionSpec as P

MESH = pl.DeviceIdType.MESH
F32 = jnp.float32
BF16 = jnp.bfloat16
TILE = 8
LANES = 128
BAND = 64
MIB = 2**20


def wrap(value, size):
    return jnp.where(value >= size, value - size, value)


def unit_rows(wide):
    mean = jnp.sum(wide * wide, axis=1, keepdims=True) * (1.0 / wide.shape[1])
    return wide * lax.rsqrt(mean + 1e-06)


def each(first, last, body):
    def run(k, carry):
        body(k)
        return carry

    lax.fori_loop(first, last, run, 0)


def gram_kernel(
    n_rows, n_cols, env_total, block,
    pick_ref, count_ref, atoms_ref, sparse_ref, x_ref,
    rows_ref, whole_ref, sum_ref,
    xbuf, kbuf, partial, factor, columns, units, gathered, zbuf, gram, gbuf, total_gram, cross, cbuf,
    picks, count, xsem, osem, isem, zsend, zrecv, psend, fsend, precv, gsend, csend, wsend, rsem,
):
    me = lax.axis_index("rows")
    group = lax.axis_index("cols")
    chip, core = me // 2, lax.rem(me, 2)
    n_chips = n_rows // 2
    slots, depth = xbuf.shape
    width, panel = units.shape[0], gathered.shape[0]
    half, short = depth // 2, width // 2

    def rows_of(i, size):
        return pl.ds(pl.multiple_of(i * size, size), size)

    load_units = pltpu.make_async_copy(sparse_ref, units, isem.at[0])
    load_picks = pltpu.make_async_copy(pick_ref, picks, isem.at[1])
    load_count = pltpu.make_async_copy(count_ref, count, isem.at[2])
    load_units.start()
    load_picks.start()
    load_count.start()
    def load(i):
        at = rows_of(i, block)
        return pltpu.make_async_copy(x_ref.at[at, :], xbuf.at[at, :], xsem.at[i])

    each(0, slots // block, lambda i: load(i).start())

    barrier = pltpu.get_barrier_semaphore()
    each(1, n_rows, lambda k: pl.semaphore_signal(
        barrier, inc=1, device_id=(wrap(me + k, n_rows), group), device_id_type=MESH))
    for k in range(1, n_cols):
        pl.semaphore_signal(
            barrier, inc=1, device_id=(me, wrap(group + k, n_cols)), device_id_type=MESH
        )

    load_units.wait()

    load_picks.wait()
    column = lax.broadcasted_iota(jnp.int32, (16, width), 1) + group * width
    row = lax.broadcasted_iota(jnp.int32, (16, width), 0)
    wanted = jnp.zeros((16, width), jnp.int32)
    for i in range(16):
        wanted = jnp.where(row == i, picks[chip * 16 + i], wanted)
    one_hot = jnp.where(wanted == column, 1.0, 0.0).astype(BF16)
    chosen = unit_rows(jnp.dot(one_hot, units[...], preferred_element_type=F32))
    zbuf[group] = jnp.where(core == 0, chosen[:, :half], chosen[:, half:]).astype(BF16)

    def z_copy(k):
        return pltpu.make_async_remote_copy(
            src_ref=zbuf.at[group], dst_ref=zbuf.at[group],
            send_sem=zsend.at[k - 1], recv_sem=zrecv.at[k - 1],
            device_id=(me, wrap(group + k, n_cols)), device_id_type=MESH,
        )

    pl.semaphore_wait(barrier, n_rows - 1 + n_cols - 1)
    for k in range(1, n_cols):
        z_copy(k).start()

    for i in range(0, width, 128):
        units[i : i + 128, :] = unit_rows(units[i : i + 128, :].astype(F32)).astype(BF16)
    load_count.wait()
    weight = (8.0 * lax.rsqrt(atoms_ref[...].astype(F32))).astype(BF16).astype(F32)
    slot = (
        lax.broadcasted_iota(jnp.int32, atoms_ref.shape, 0) * LANES
        + lax.broadcasted_iota(jnp.int32, atoms_ref.shape, 1)
    )
    roots = jnp.where(slot < count[0], jnp.sqrt(weight * (1.0 / depth)), 0.0).T
    lines = block // LANES
    blocks = slots // block
    for i in range(blocks):
        columns[i] = roots[:, i * lines : (i + 1) * lines]

    def save(i):
        at = rows_of(i, block)
        return pltpu.make_async_copy(
            kbuf.at[at, pl.ds(0, width)], rows_ref.at[at, :], osem.at[i]
        )

    def norms(first, last):
        each(first, last, lambda i: load(i).wait())
        at = slice(first * block, last * block)
        wide = xbuf[at, :].astype(F32)
        mean = jnp.sum(wide * wide, axis=1, keepdims=True) * (1.0 / depth)
        root = jnp.concatenate(
            [columns[i][:, j : j + 1] for i in range(first, last) for j in range(lines)], axis=0
        )
        factor[at, :] = jnp.broadcast_to(
            root * lax.rsqrt(mean + 1e-06), ((last - first) * block, LANES)
        )

    def kernel_of(at, points):
        inner = lax.dot_general(
            xbuf[at, :], points[...], (((1,), (1,)), ((), ())), preferred_element_type=F32
        ) * jnp.concatenate([factor[at, :]] * (points.shape[0] // LANES), axis=1)
        return (inner * inner).astype(BF16)

    def own_points(first, last):
        at = slice(first * block, last * block)
        kbuf[at, :width] = kernel_of(at, units)
        each(first, last, lambda i: save(i).start())

    def panel_half(at, which):
        across = rows_of(which, half)
        return lax.dot_general(
            xbuf[at, across], gathered[:, across], (((1,), (1,)), ((), ())),
            preferred_element_type=F32,
        )

    def panel_points(at):
        inner = partial[at, :] + panel_half(at, 1 - core)
        inner = inner * jnp.concatenate([factor[at, :]] * (panel // LANES), axis=1)
        kbuf[at, width:] = (inner * inner).astype(BF16)

    third = blocks // 3
    late = 2 * third
    norms(0, third)
    own_points(0, third)

    for k in range(1, n_cols):
        z_copy(k).wait()
    total = zbuf[0].astype(F32)
    for k in range(1, n_cols):
        total = total + zbuf[k].astype(F32)

    def piece(which_chip, which_core):
        return gathered.at[rows_of(which_chip, 16), rows_of(which_core, half)]

    piece(chip, core)[...] = total.astype(BF16)

    def plane_copy(k):
        return pltpu.make_async_remote_copy(
            src_ref=piece(chip, core), dst_ref=piece(chip, core),
            send_sem=psend.at[k], recv_sem=precv.at[core, chip],
            device_id=(wrap(chip + k, n_chips) * 2 + core, group), device_id_type=MESH,
        )

    def core_copy(source):
        return pltpu.make_async_remote_copy(
            src_ref=piece(source, core), dst_ref=piece(source, core),
            send_sem=fsend.at[source], recv_sem=precv.at[core, source],
            device_id=(chip * 2 + 1 - core, group), device_id_type=MESH,
        )

    def arrival(source, which_core):
        return pltpu.make_async_copy(
            piece(source, which_core), piece(source, which_core), precv.at[which_core, source]
        )

    each(1, n_chips, lambda k: plane_copy(k).start())
    core_copy(chip).start()
    norms(third, late)
    own_points(third, late)
    norms(late, blocks)
    own_points(late, blocks)

    def forward(k):
        source = wrap(chip + n_chips - k, n_chips)
        arrival(source, core).wait()
        core_copy(source).start()

    each(1, n_chips, forward)

    parts = [slice(i * slots // 3, (i + 1) * slots // 3) for i in range(3)]
    for at in parts:
        partial[at, :] = panel_half(at, core)

    def finish(k):
        source = wrap(chip + n_chips - k, n_chips)
        arrival(source, 1 - core).wait()

    each(0, n_chips, finish)
    for at in parts:
        panel_points(at)

    def transposed_product(right):
        return lax.dot_general(
            kbuf[:, width:], right, (((0,), (0,)), ((), ())), preferred_element_type=F32
        ) * (1.0 / env_total)

    gram[...] = transposed_product(kbuf[:, width:])

    def gram_copy(k):
        peer = wrap(me + k, n_rows)
        return pltpu.make_async_remote_copy(
            src_ref=gram.at[rows_of(peer, TILE), :], dst_ref=gbuf.at[k - 1],
            send_sem=gsend.at[k], recv_sem=rsem.at[0],
            device_id=(peer, group), device_id_type=MESH,
        )

    def cross_copy(k):
        peer = wrap(me + k, n_rows)
        return pltpu.make_async_remote_copy(
            src_ref=cross.at[peer], dst_ref=cbuf.at[k - 1],
            send_sem=csend.at[k], recv_sem=rsem.at[1],
            device_id=(peer, group), device_id_type=MESH,
        )

    def whole_copy(k):
        return pltpu.make_async_remote_copy(
            src_ref=total_gram.at[rows_of(me, TILE), :],
            dst_ref=total_gram.at[rows_of(me, TILE), :],
            send_sem=wsend.at[k], recv_sem=rsem.at[2],
            device_id=(wrap(me + k, n_rows), group), device_id_type=MESH,
        )

    each(1, n_rows, lambda k: gram_copy(k).start())
    product = transposed_product(kbuf[:, :width])
    for r in range(panel // TILE):
        part = product[r * TILE : (r + 1) * TILE, :]
        cross[r] = jnp.concatenate([part[:, :short], part[:, short:]], axis=0).astype(BF16)
    each(1, n_rows, lambda k: cross_copy(k).start())
    pltpu.make_async_copy(gbuf, gbuf, rsem.at[0]).wait()
    total = gram[rows_of(me, TILE), :]
    for r in range(n_rows - 1):
        total = total + gbuf[r]
    total_gram[rows_of(me, TILE), :] = total
    each(1, n_rows, lambda k: whole_copy(k).start())
    pltpu.make_async_copy(cbuf, cbuf, rsem.at[1]).wait()
    total = cross[me].astype(F32)
    for r in range(n_rows - 1):
        total = total + cbuf[r].astype(F32)
    sum_ref[:, :short] = total[:TILE]
    sum_ref[:, short:] = total[TILE:]
    arrived = total_gram.at[pl.ds(0, panel - TILE), :]
    pltpu.make_async_copy(arrived, arrived, rsem.at[2]).wait()
    whole_ref[...] = total_gram[...]

    def all_sent(k):
        gram_copy(k).wait_send()
        cross_copy(k).wait_send()
        whole_copy(k).wait_send()

    each(1, n_rows, all_sent)
    each(1, n_chips, lambda k: plane_copy(k).wait_send())
    each(0, n_chips, lambda k: core_copy(k).wait_send())
    each(0, blocks, lambda i: save(i).wait())


def gram_pass(panel_pick, env_count, struct_atoms, sparse_desc, descriptors, n_rows, n_cols, block):
    slots, depth = descriptors.shape
    width, panel = sparse_desc.shape[0], panel_pick.shape[0]
    n_chips = n_rows // 2
    short = width // 2
    hbm = pl.BlockSpec(memory_space=pl.ANY)
    vmem = pl.BlockSpec(memory_space=pltpu.VMEM)
    dma = pltpu.SemaphoreType.DMA
    return pl.pallas_call(
        functools.partial(gram_kernel, n_rows, n_cols, slots // 3 * n_rows, block),
        out_shape=(
            jax.ShapeDtypeStruct((slots, width), BF16),
            jax.ShapeDtypeStruct((panel, panel), F32),
            jax.ShapeDtypeStruct((TILE, width), F32),
        ),
        in_specs=[hbm, hbm, vmem, hbm, hbm],
        out_specs=(hbm, vmem, vmem),
        scratch_shapes=[
            pltpu.VMEM((slots, depth), BF16),
            pltpu.VMEM((slots, width + panel), BF16),
            pltpu.VMEM((slots, panel), F32),
            pltpu.VMEM((slots, LANES), F32),
            pltpu.VMEM((slots // block, LANES, block // LANES), F32),
            pltpu.VMEM((width, depth), BF16),
            pltpu.VMEM((panel, depth), BF16),
            pltpu.VMEM((n_cols, 16, depth // 2), BF16),
            pltpu.VMEM((panel, panel), F32),
            pltpu.VMEM((n_rows - 1, TILE, panel), F32),
            pltpu.VMEM((panel, panel), F32),
            pltpu.VMEM((n_rows, 2 * TILE, short), BF16),
            pltpu.VMEM((n_rows - 1, 2 * TILE, short), BF16),
            pltpu.SMEM((panel,), jnp.int32),
            pltpu.SMEM((1,), jnp.int32),
            dma((slots // block,)),
            dma((slots // block,)),
            dma((3,)),
            dma((n_cols - 1,)),
            dma((n_cols - 1,)),
            dma((n_chips,)),
            dma((n_chips,)),
            dma((2, n_chips)),
            dma((n_rows,)),
            dma((n_rows,)),
            dma((n_rows,)),
            dma((3,)),
        ],
        compiler_params=pltpu.CompilerParams(
            collective_id=0, has_side_effects=True, vmem_limit_bytes=56 * MIB
        ),
        name="gram_pass",
    )(panel_pick, env_count, struct_atoms.reshape(slots // LANES, LANES), sparse_desc, descriptors)


def wide_of(tile, lane):
    return jnp.broadcast_to(tile[:, lane : lane + 1], (TILE, LANES))


def tall_of(tile, line):
    return jnp.broadcast_to(tile[line : line + 1, :], (TILE, LANES))


def factor_band(tiles, first):
    groups, halves = len(tiles), len(tiles[0])
    line = lax.broadcasted_iota(jnp.int32, (TILE, LANES), 0)
    out = []
    for t in range(groups):
        base = first + t * TILE
        cols = {g: [wide_of(tiles[g][0], base + k) for k in range(TILE)] for g in range(t, groups)}
        low = {(i, k): tall_of(cols[t][k], i) for k in range(TILE) for i in range(k, TILE)}
        inv = []
        for k in range(0, TILE, 2):
            top, mixed, bottom = low[k, k], low[k + 1, k], low[k + 1, k + 1]
            root = lax.rsqrt(top)
            inv.append(root)
            inv.append(top * root * lax.rsqrt(top * bottom - mixed * mixed))
            for i in range(k + 1, TILE):
                low[i, k] = low[i, k] * root
            for i in range(k + 2, TILE):
                low[i, k + 1] = (low[i, k + 1] - low[i, k] * low[k + 1, k]) * inv[k + 1]
            for m in range(k + 2, TILE):
                for i in range(m, TILE):
                    low[i, m] = low[i, m] - (low[i, k] * low[m, k] + low[i, k + 1] * low[m, k + 1])
        band = []
        for h in range(halves):
            lines = []
            for k in range(TILE):
                value = tall_of(tiles[t][h], k)
                for m in range(k):
                    value = value - low[k, m] * lines[m]
                lines.append(value * inv[k])
            band.append(lines)
        merged = []
        for h in range(halves):
            value = band[h][0]
            for k in range(1, TILE):
                value = jnp.where(line == k, band[h][k], value)
            merged.append(value)
        out.append(merged)
        for g in range(t + 1, groups):
            left = []
            for k in range(TILE):
                value = cols[g][k]
                for m in range(k):
                    value = value - left[m] * low[k, m]
                left.append(value * inv[k])
            for h in range(halves):
                terms = [left[k] * band[h][k] for k in range(TILE)]
                while len(terms) > 1:
                    terms = [x + y for x, y in zip(terms[::2], terms[1::2], strict=True)]
                tiles[g][h] = tiles[g][h] - terms[0]
    return out


def factor_kernel(
    gram_ref, rows_ref, sum_ref, out_ref, kernel_ref, cross_ref, work, passing, sums, isem, osem
):
    size = gram_ref.shape[0]
    parts = osem.shape[0] - 1
    part = rows_ref.shape[0] // parts
    chunks = [pl.ds(i * part, part) for i in range(parts)]
    load = pltpu.make_async_copy(gram_ref, work, isem.at[parts])
    loads = [
        pltpu.make_async_copy(rows_ref.at[c, :], passing.at[c, :], isem.at[i])
        for i, c in enumerate(chunks)
    ]
    loads.append(pltpu.make_async_copy(sum_ref, sums, isem.at[parts + 1]))
    saves = [
        pltpu.make_async_copy(passing.at[c, :], kernel_ref.at[c, :], osem.at[i])
        for i, c in enumerate(chunks)
    ]
    saves.append(pltpu.make_async_copy(sums, cross_ref, osem.at[parts]))
    load.start()
    for copy in loads:
        copy.start()
    load.wait()
    halves = size // LANES
    line = lax.broadcasted_iota(jnp.int32, (TILE, LANES), 0)
    lane = lax.broadcasted_iota(jnp.int32, (TILE, LANES), 1)

    def tile(g, h):
        return slice(g * TILE, (g + 1) * TILE), slice(h * LANES, (h + 1) * LANES)

    tall, wide, diagonal = [], [], []
    for h in range(halves):
        along = jnp.zeros((TILE, LANES), F32)
        for g in range(h * LANES // TILE, (h + 1) * LANES // TILE):
            there = jnp.where(lane == line + (g * TILE - h * LANES), work[tile(g, h)], 0.0)
            tall.append(lax.rsqrt(jnp.sum(there, axis=1, keepdims=True)))
            along = along + there
        diagonal.append(jnp.sum(along, axis=0, keepdims=True))
        wide.append(lax.rsqrt(diagonal[h]))
    for g in range(size // TILE):
        for h in range(g * TILE // LANES, halves):
            work[tile(g, h)] = work[tile(g, h)] * tall[g] * wide[h]
    for start in range(0, size, BAND):
        end, near = start + BAND, start // LANES
        tiles = [
            [work[tile(g, h)] for h in range(near, halves)]
            for g in range(start // TILE, end // TILE)
        ]
        factor = factor_band(tiles, start % LANES)
        for i, parts_of in enumerate(factor):
            g = start // TILE + i
            for h in range(halves):
                value = jnp.zeros((TILE, LANES), F32) if h < near else parts_of[h - near]
                if h == near:
                    value = jnp.where(lane >= line + (g * TILE - h * LANES), value, 0.0)
                work[tile(g, h)] = value
        if start == 0:
            for copy, then in zip(loads, saves, strict=True):
                copy.wait()
                then.start()
        if end < size:
            far = end // LANES * LANES
            right = work[start:end, far:]
            inner = lax.dot_general(
                right, right, (((0,), (0,)), ((), ())),
                precision=lax.Precision.HIGHEST, preferred_element_type=F32,
            )
            work[end:, far:] -= inner[end - far :, :]
    me = lax.axis_index("rows")
    out_ref[...] = work[pl.ds(pl.multiple_of(me * TILE, TILE), TILE), :] * jnp.concatenate(
        [diagonal[h] * wide[h] for h in range(halves)], axis=1
    )
    for copy in saves:
        copy.wait()


def factor_pass(gram, kernel_rows, cross_sum):
    size = gram.shape[0]
    hbm = pl.BlockSpec(memory_space=pl.ANY)
    vmem = pl.BlockSpec(memory_space=pltpu.VMEM)
    return pl.pallas_call(
        factor_kernel,
        out_shape=(
            jax.ShapeDtypeStruct((TILE, size), F32),
            jax.ShapeDtypeStruct(kernel_rows.shape, BF16),
            jax.ShapeDtypeStruct(cross_sum.shape, F32),
        ),
        in_specs=[hbm, hbm, hbm],
        out_specs=(vmem, hbm, hbm),
        scratch_shapes=[
            pltpu.VMEM((size, size), F32),
            pltpu.VMEM(kernel_rows.shape, BF16),
            pltpu.VMEM(cross_sum.shape, F32),
            pltpu.SemaphoreType.DMA((8,)),
            pltpu.SemaphoreType.DMA((7,)),
        ],
        compiler_params=pltpu.CompilerParams(vmem_limit_bytes=60 * MIB),
        name="factor_pass",
    )(gram, kernel_rows, cross_sum)


def local(descriptors, struct_atoms, env_count, sparse_desc, panel_pick):
    n_rows, n_cols = lax.axis_size("rows"), lax.axis_size("cols")
    kernel_rows, gram, cross_sum = gram_pass(
        panel_pick, env_count, struct_atoms, sparse_desc, descriptors, n_rows, n_cols, 512
    )
    factor_rows, kernel_rows, cross_gram = factor_pass(gram, kernel_rows, cross_sum)
    return kernel_rows, factor_rows, cross_gram


def solution(mesh):
    return jax.shard_map(
        local,
        mesh=mesh,
        in_specs=(P("rows", None), P("rows"), P("rows"), P("cols", None), P()),
        out_specs=(P("rows", "cols"), P("rows", None), P("rows", "cols")),
        check_vma=False,
    )
```

```python
import functools

import jax
import jax.numpy as jnp
from jax import lax
from jax.experimental import pallas as pl
from jax.experimental.pallas import tpu as pltpu
from jax.sharding import PartitionSpec as P

MESH = pl.DeviceIdType.MESH
F32 = jnp.float32
BF16 = jnp.bfloat16
TILE = 8
LANES = 128
BAND = 64
MIB = 2**20


def wrap(value, size):
    return jnp.where(value >= size, value - size, value)


def unit_rows(wide):
    mean = jnp.sum(wide * wide, axis=1, keepdims=True) * (1.0 / wide.shape[1])
    return wide * lax.rsqrt(mean + 1e-06)


def each(first, last, body):
    def run(k, carry):
        body(k)
        return carry

    lax.fori_loop(first, last, run, 0)


def gram_kernel(
    n_rows, n_cols, env_total, block,
    pick_ref, count_ref, atoms_ref, sparse_ref, x_ref,
    rows_ref, whole_ref, sum_ref,
    xbuf, kbuf, partial, factor, columns, units, gathered, zbuf, gram, gbuf, lbuf, total_gram, cross, cbuf, sumbuf,
    picks, count, xsem, osem, isem, zsend, zrecv, psend, fsend, precv, gsend, csend, wsend, lsend, vsend, rsem,
):
    me = lax.axis_index("rows")
    group = lax.axis_index("cols")
    chip, core = me // 2, lax.rem(me, 2)
    n_chips = n_rows // 2
    slots, depth = xbuf.shape
    width, panel = units.shape[0], gathered.shape[0]
    half, short = depth // 2, width // 2

    def rows_of(i, size):
        return pl.ds(pl.multiple_of(i * size, size), size)

    load_units = pltpu.make_async_copy(sparse_ref, units, isem.at[0])
    load_picks = pltpu.make_async_copy(pick_ref, picks, isem.at[1])
    load_count = pltpu.make_async_copy(count_ref, count, isem.at[2])
    load_units.start()
    load_picks.start()
    load_count.start()
    def load(i):
        at = rows_of(i, block)
        return pltpu.make_async_copy(x_ref.at[at, :], xbuf.at[at, :], xsem.at[i])

    each(0, slots // block, lambda i: load(i).start())

    barrier = pltpu.get_barrier_semaphore()
    each(1, n_rows, lambda k: pl.semaphore_signal(
        barrier, inc=1, device_id=(wrap(me + k, n_rows), group), device_id_type=MESH))
    for k in range(1, n_cols):
        pl.semaphore_signal(
            barrier, inc=1, device_id=(me, wrap(group + k, n_cols)), device_id_type=MESH
        )

    load_units.wait()

    load_picks.wait()
    column = lax.broadcasted_iota(jnp.int32, (16, width), 1) + group * width
    row = lax.broadcasted_iota(jnp.int32, (16, width), 0)
    wanted = jnp.zeros((16, width), jnp.int32)
    for i in range(16):
        wanted = jnp.where(row == i, picks[chip * 16 + i], wanted)
    one_hot = jnp.where(wanted == column, 1.0, 0.0).astype(BF16)
    chosen = unit_rows(jnp.dot(one_hot, units[...], preferred_element_type=F32))
    zbuf[group] = jnp.where(core == 0, chosen[:, :half], chosen[:, half:]).astype(BF16)

    def z_copy(k):
        return pltpu.make_async_remote_copy(
            src_ref=zbuf.at[group], dst_ref=zbuf.at[group],
            send_sem=zsend.at[k - 1], recv_sem=zrecv.at[k - 1],
            device_id=(me, wrap(group + k, n_cols)), device_id_type=MESH,
        )

    pl.semaphore_wait(barrier, n_rows - 1 + n_cols - 1)
    for k in range(1, n_cols):
        z_copy(k).start()

    for i in range(0, width, 128):
        units[i : i + 128, :] = unit_rows(units[i : i + 128, :].astype(F32)).astype(BF16)
    load_count.wait()
    weight = (8.0 * lax.rsqrt(atoms_ref[...].astype(F32))).astype(BF16).astype(F32)
    slot = (
        lax.broadcasted_iota(jnp.int32, atoms_ref.shape, 0) * LANES
        + lax.broadcasted_iota(jnp.int32, atoms_ref.shape, 1)
    )
    roots = jnp.where(slot < count[0], jnp.sqrt(weight * (1.0 / depth)), 0.0).T
    lines = block // LANES
    blocks = slots // block
    for i in range(blocks):
        columns[i] = roots[:, i * lines : (i + 1) * lines]

    def save(i):
        at = rows_of(i, block)
        return pltpu.make_async_copy(
            kbuf.at[at, pl.ds(0, width)], rows_ref.at[at, :], osem.at[i]
        )

    def norms(first, last):
        each(first, last, lambda i: load(i).wait())
        at = slice(first * block, last * block)
        wide = xbuf[at, :].astype(F32)
        mean = jnp.sum(wide * wide, axis=1, keepdims=True) * (1.0 / depth)
        root = jnp.concatenate(
            [columns[i][:, j : j + 1] for i in range(first, last) for j in range(lines)], axis=0
        )
        factor[at, :] = jnp.broadcast_to(
            root * lax.rsqrt(mean + 1e-06), ((last - first) * block, LANES)
        )

    def kernel_of(at, points):
        inner = lax.dot_general(
            xbuf[at, :], points[...], (((1,), (1,)), ((), ())), preferred_element_type=F32
        ) * jnp.concatenate([factor[at, :]] * (points.shape[0] // LANES), axis=1)
        return (inner * inner).astype(BF16)

    def own_points(first, last):
        at = slice(first * block, last * block)
        kbuf[at, :width] = kernel_of(at, units)
        each(first, last, lambda i: save(i).start())

    def panel_half(at, which):
        across = rows_of(which, half)
        return lax.dot_general(
            xbuf[at, across], gathered[:, across], (((1,), (1,)), ((), ())),
            preferred_element_type=F32,
        )

    def panel_points(at):
        inner = partial[at, :] + panel_half(at, 1 - core)
        inner = inner * jnp.concatenate([factor[at, :]] * (panel // LANES), axis=1)
        kbuf[at, width:] = (inner * inner).astype(BF16)

    third = blocks // 3
    late = 2 * third
    norms(0, third)
    own_points(0, third)

    for k in range(1, n_cols):
        z_copy(k).wait()
    total = zbuf[0].astype(F32)
    for k in range(1, n_cols):
        total = total + zbuf[k].astype(F32)

    def piece(which_chip, which_core):
        return gathered.at[rows_of(which_chip, 16), rows_of(which_core, half)]

    piece(chip, core)[...] = total.astype(BF16)

    def plane_copy(k):
        return pltpu.make_async_remote_copy(
            src_ref=piece(chip, core), dst_ref=piece(chip, core),
            send_sem=psend.at[k], recv_sem=precv.at[core, chip],
            device_id=(wrap(chip + k, n_chips) * 2 + core, group), device_id_type=MESH,
        )

    def core_copy(source):
        return pltpu.make_async_remote_copy(
            src_ref=piece(source, core), dst_ref=piece(source, core),
            send_sem=fsend.at[source], recv_sem=precv.at[core, source],
            device_id=(chip * 2 + 1 - core, group), device_id_type=MESH,
        )

    def arrival(source, which_core):
        return pltpu.make_async_copy(
            piece(source, which_core), piece(source, which_core), precv.at[which_core, source]
        )

    each(1, n_chips, lambda k: plane_copy(k).start())
    core_copy(chip).start()
    norms(third, late)
    own_points(third, late)
    norms(late, blocks)
    own_points(late, blocks)

    def forward(k):
        source = wrap(chip + n_chips - k, n_chips)
        arrival(source, core).wait()
        core_copy(source).start()

    each(1, n_chips, forward)

    parts = [slice(i * slots // 3, (i + 1) * slots // 3) for i in range(3)]
    for at in parts:
        partial[at, :] = panel_half(at, core)

    def finish(k):
        source = wrap(chip + n_chips - k, n_chips)
        arrival(source, 1 - core).wait()

    each(0, n_chips, finish)
    for at in parts:
        panel_points(at)

    def transposed_product(right):
        return lax.dot_general(
            kbuf[:, width:], right, (((0,), (0,)), ((), ())), preferred_element_type=F32
        ) * (1.0 / env_total)

    gram[...] = transposed_product(kbuf[:, width:])

    low, high = pl.ds(0, panel // 2), pl.ds(panel // 2, panel // 2)

    def right_copy(k):
        peer = wrap(me + k, n_rows)
        return pltpu.make_async_remote_copy(
            src_ref=gram.at[rows_of(peer, TILE), high], dst_ref=gbuf.at[me],
            send_sem=gsend.at[k], recv_sem=rsem.at[0],
            device_id=(peer, group), device_id_type=MESH,
        )

    def left_copy(k):
        to_chip = wrap(chip + k, n_chips)
        return pltpu.make_async_remote_copy(
            src_ref=gram.at[rows_of(to_chip, TILE), low], dst_ref=lbuf.at[me],
            send_sem=lsend.at[k], recv_sem=rsem.at[3],
            device_id=(to_chip * 2, group), device_id_type=MESH,
        )

    def cross_copy(k):
        peer = wrap(me + k, n_rows)
        return pltpu.make_async_remote_copy(
            src_ref=cross.at[peer], dst_ref=cbuf.at[k - 1],
            send_sem=csend.at[k], recv_sem=rsem.at[1],
            device_id=(peer, group), device_id_type=MESH,
        )

    def right_whole(k):
        mine = total_gram.at[rows_of(me, TILE), high]
        return pltpu.make_async_remote_copy(
            src_ref=mine, dst_ref=mine, send_sem=wsend.at[k], recv_sem=rsem.at[2],
            device_id=(wrap(me + k, n_rows), group), device_id_type=MESH,
        )

    def left_whole(k):
        mine = total_gram.at[rows_of(chip, TILE), low]
        return pltpu.make_async_remote_copy(
            src_ref=mine, dst_ref=mine, send_sem=vsend.at[k], recv_sem=rsem.at[4],
            device_id=(wrap(me + k, n_rows), group), device_id_type=MESH,
        )

    def landed(ref, sem):
        pltpu.make_async_copy(ref, ref, sem).wait()

    each(1, n_rows, lambda k: right_copy(k).start())
    each(1, n_chips, lambda k: left_copy(k).start())

    @pl.when(core == 1)
    def _():
        left_copy(0).start()

    total_gram[panel // 2 :, : panel // 2] = jnp.zeros((panel // 2, panel // 2), F32)
    gbuf[me] = gram[rows_of(me, TILE), panel // 2 :]
    lbuf[me] = gram[rows_of(chip, TILE), : panel // 2]
    product = transposed_product(kbuf[:, :width])
    for r in range(panel // TILE):
        part = product[r * TILE : (r + 1) * TILE, :]
        cross[r] = jnp.concatenate([part[:, :short], part[:, short:]], axis=0).astype(BF16)
    each(1, n_rows, lambda k: cross_copy(k).start())

    def summed(pieces):
        total = pieces[0]
        for r in range(1, n_rows):
            total = total + pieces[r]
        return total

    others = pl.ds(0, n_rows - 1)
    landed(gbuf.at[others], rsem.at[0])
    total_gram[rows_of(me, TILE), panel // 2 :] = summed(gbuf)
    each(1, n_rows, lambda k: right_whole(k).start())

    @pl.when(core == 0)
    def _():
        landed(lbuf.at[others], rsem.at[3])
        total_gram[rows_of(chip, TILE), : panel // 2] = summed(lbuf)
        each(1, n_rows, lambda k: left_whole(k).start())

    pltpu.make_async_copy(cbuf, cbuf, rsem.at[1]).wait()
    total = cross[me].astype(F32)
    for r in range(n_rows - 1):
        total = total + cbuf[r].astype(F32)
    sumbuf[:, :short] = total[:TILE]
    sumbuf[:, short:] = total[TILE:]
    save_sum = pltpu.make_async_copy(sumbuf, sum_ref, isem.at[3])
    save_sum.start()

    def early_sent(k):
        right_copy(k).wait_send()
        cross_copy(k).wait_send()

    each(1, n_rows, early_sent)
    each(1, n_chips, lambda k: left_copy(k).wait_send())
    each(1, n_chips, lambda k: plane_copy(k).wait_send())
    each(0, n_chips, lambda k: core_copy(k).wait_send())
    each(0, blocks, lambda i: save(i).wait())
    landed(total_gram.at[pl.ds(0, panel - TILE), high], rsem.at[2])

    @pl.when(core == 0)
    def _():
        landed(total_gram.at[pl.ds(0, (n_chips - 1) * TILE), low], rsem.at[4])

    @pl.when(core == 1)
    def _():
        landed(total_gram.at[pl.ds(0, n_chips * TILE), low], rsem.at[4])

    save_whole = pltpu.make_async_copy(total_gram, whole_ref, isem.at[4])
    save_whole.start()

    @pl.when(core == 1)
    def _():
        left_copy(0).wait_send()

    @pl.when(core == 0)
    def _():
        each(1, n_rows, lambda k: left_whole(k).wait_send())

    each(1, n_rows, lambda k: right_whole(k).wait_send())
    save_sum.wait()
    save_whole.wait()


def gram_pass(panel_pick, env_count, struct_atoms, sparse_desc, descriptors, n_rows, n_cols, block):
    slots, depth = descriptors.shape
    width, panel = sparse_desc.shape[0], panel_pick.shape[0]
    n_chips = n_rows // 2
    short = width // 2
    hbm = pl.BlockSpec(memory_space=pl.ANY)
    vmem = pl.BlockSpec(memory_space=pltpu.VMEM)
    dma = pltpu.SemaphoreType.DMA
    return pl.pallas_call(
        functools.partial(gram_kernel, n_rows, n_cols, slots // 3 * n_rows, block),
        out_shape=(
            jax.ShapeDtypeStruct((slots, width), BF16),
            jax.ShapeDtypeStruct((panel, panel), F32),
            jax.ShapeDtypeStruct((TILE, width), F32),
        ),
        in_specs=[hbm, hbm, vmem, hbm, hbm],
        out_specs=(hbm, hbm, hbm),
        scratch_shapes=[
            pltpu.VMEM((slots, depth), BF16),
            pltpu.VMEM((slots, width + panel), BF16),
            pltpu.VMEM((slots, panel), F32),
            pltpu.VMEM((slots, LANES), F32),
            pltpu.VMEM((slots // block, LANES, block // LANES), F32),
            pltpu.VMEM((width, depth), BF16),
            pltpu.VMEM((panel, depth), BF16),
            pltpu.VMEM((n_cols, 16, depth // 2), BF16),
            pltpu.VMEM((panel, panel), F32),
            pltpu.VMEM((n_rows, TILE, panel // 2), F32),
            pltpu.VMEM((n_rows, TILE, panel // 2), F32),
            pltpu.VMEM((panel, panel), F32),
            pltpu.VMEM((n_rows, 2 * TILE, short), BF16),
            pltpu.VMEM((n_rows - 1, 2 * TILE, short), BF16),
            pltpu.VMEM((TILE, width), F32),
            pltpu.SMEM((panel,), jnp.int32),
            pltpu.SMEM((1,), jnp.int32),
            dma((slots // block,)),
            dma((slots // block,)),
            dma((5,)),
            dma((n_cols - 1,)),
            dma((n_cols - 1,)),
            dma((n_chips,)),
            dma((n_chips,)),
            dma((2, n_chips)),
            dma((n_rows,)),
            dma((n_rows,)),
            dma((n_rows,)),
            dma((n_chips,)),
            dma((n_rows,)),
            dma((5,)),
        ],
        compiler_params=pltpu.CompilerParams(
            collective_id=0, has_side_effects=True, vmem_limit_bytes=56 * MIB
        ),
        name="gram_pass",
    )(panel_pick, env_count, struct_atoms.reshape(slots // LANES, LANES), sparse_desc, descriptors)


def wide_of(tile, lane):
    return jnp.broadcast_to(tile[:, lane : lane + 1], (TILE, LANES))


def tall_of(tile, line):
    return jnp.broadcast_to(tile[line : line + 1, :], (TILE, LANES))


def factor_band(tiles, first):
    groups, halves = len(tiles), len(tiles[0])
    line = lax.broadcasted_iota(jnp.int32, (TILE, LANES), 0)
    out = []
    for t in range(groups):
        base = first + t * TILE
        cols = {g: [wide_of(tiles[g][0], base + k) for k in range(TILE)] for g in range(t, groups)}
        low = {(i, k): tall_of(cols[t][k], i) for k in range(TILE) for i in range(k, TILE)}
        inv = []
        for k in range(0, TILE, 2):
            top, mixed, bottom = low[k, k], low[k + 1, k], low[k + 1, k + 1]
            root = lax.rsqrt(top)
            inv.append(root)
            inv.append(top * root * lax.rsqrt(top * bottom - mixed * mixed))
            for i in range(k + 1, TILE):
                low[i, k] = low[i, k] * root
            for i in range(k + 2, TILE):
                low[i, k + 1] = (low[i, k + 1] - low[i, k] * low[k + 1, k]) * inv[k + 1]
            for m in range(k + 2, TILE):
                for i in range(m, TILE):
                    low[i, m] = low[i, m] - (low[i, k] * low[m, k] + low[i, k + 1] * low[m, k + 1])
        band = []
        for h in range(halves):
            lines = []
            for k in range(TILE):
                value = tall_of(tiles[t][h], k)
                for m in range(k):
                    value = value - low[k, m] * lines[m]
                lines.append(value * inv[k])
            band.append(lines)
        merged = []
        for h in range(halves):
            value = band[h][0]
            for k in range(1, TILE):
                value = jnp.where(line == k, band[h][k], value)
            merged.append(value)
        out.append(merged)
        for g in range(t + 1, groups):
            left = []
            for k in range(TILE):
                value = cols[g][k]
                for m in range(k):
                    value = value - left[m] * low[k, m]
                left.append(value * inv[k])
            for h in range(halves):
                terms = [left[k] * band[h][k] for k in range(TILE)]
                while len(terms) > 1:
                    terms = [x + y for x, y in zip(terms[::2], terms[1::2], strict=True)]
                tiles[g][h] = tiles[g][h] - terms[0]
    return out


def factor_kernel(
    gram_ref, rows_ref, sum_ref, out_ref, kernel_ref, cross_ref, work, passing, sums, isem, osem
):
    size = gram_ref.shape[0]
    parts = osem.shape[0] - 1
    part = rows_ref.shape[0] // parts
    chunks = [pl.ds(i * part, part) for i in range(parts)]
    load = pltpu.make_async_copy(gram_ref, work, isem.at[parts])
    loads = [
        pltpu.make_async_copy(rows_ref.at[c, :], passing.at[c, :], isem.at[i])
        for i, c in enumerate(chunks)
    ]
    loads.append(pltpu.make_async_copy(sum_ref, sums, isem.at[parts + 1]))
    saves = [
        pltpu.make_async_copy(passing.at[c, :], kernel_ref.at[c, :], osem.at[i])
        for i, c in enumerate(chunks)
    ]
    saves.append(pltpu.make_async_copy(sums, cross_ref, osem.at[parts]))
    load.start()
    for copy in loads:
        copy.start()
    load.wait()
    halves = size // LANES
    line = lax.broadcasted_iota(jnp.int32, (TILE, LANES), 0)
    lane = lax.broadcasted_iota(jnp.int32, (TILE, LANES), 1)

    def tile(g, h):
        return slice(g * TILE, (g + 1) * TILE), slice(h * LANES, (h + 1) * LANES)

    tall, wide, diagonal = [], [], []
    for h in range(halves):
        along = jnp.zeros((TILE, LANES), F32)
        for g in range(h * LANES // TILE, (h + 1) * LANES // TILE):
            there = jnp.where(lane == line + (g * TILE - h * LANES), work[tile(g, h)], 0.0)
            tall.append(lax.rsqrt(jnp.sum(there, axis=1, keepdims=True)))
            along = along + there
        diagonal.append(jnp.sum(along, axis=0, keepdims=True))
        wide.append(lax.rsqrt(diagonal[h]))
    for g in range(size // TILE):
        for h in range(g * TILE // LANES, halves):
            work[tile(g, h)] = work[tile(g, h)] * tall[g] * wide[h]
    for start in range(0, size, BAND):
        end, near = start + BAND, start // LANES
        tiles = [
            [work[tile(g, h)] for h in range(near, halves)]
            for g in range(start // TILE, end // TILE)
        ]
        factor = factor_band(tiles, start % LANES)
        for i, parts_of in enumerate(factor):
            g = start // TILE + i
            for h in range(halves):
                value = jnp.zeros((TILE, LANES), F32) if h < near else parts_of[h - near]
                if h == near:
                    value = jnp.where(lane >= line + (g * TILE - h * LANES), value, 0.0)
                work[tile(g, h)] = value
        if start == 0:
            for copy, then in zip(loads, saves, strict=True):
                copy.wait()
                then.start()
        if end < size:
            far = end // LANES * LANES
            right = work[start:end, far:]
            inner = lax.dot_general(
                right, right, (((0,), (0,)), ((), ())),
                precision=lax.Precision.HIGHEST, preferred_element_type=F32,
            )
            work[end:, far:] -= inner[end - far :, :]
    me = lax.axis_index("rows")
    out_ref[...] = work[pl.ds(pl.multiple_of(me * TILE, TILE), TILE), :] * jnp.concatenate(
        [diagonal[h] * wide[h] for h in range(halves)], axis=1
    )
    for copy in saves:
        copy.wait()


def factor_pass(gram, kernel_rows, cross_sum):
    size = gram.shape[0]
    hbm = pl.BlockSpec(memory_space=pl.ANY)
    vmem = pl.BlockSpec(memory_space=pltpu.VMEM)
    return pl.pallas_call(
        factor_kernel,
        out_shape=(
            jax.ShapeDtypeStruct((TILE, size), F32),
            jax.ShapeDtypeStruct(kernel_rows.shape, BF16),
            jax.ShapeDtypeStruct(cross_sum.shape, F32),
        ),
        in_specs=[hbm, hbm, hbm],
        out_specs=(vmem, hbm, hbm),
        scratch_shapes=[
            pltpu.VMEM((size, size), F32),
            pltpu.VMEM(kernel_rows.shape, BF16),
            pltpu.VMEM(cross_sum.shape, F32),
            pltpu.SemaphoreType.DMA((8,)),
            pltpu.SemaphoreType.DMA((7,)),
        ],
        compiler_params=pltpu.CompilerParams(vmem_limit_bytes=60 * MIB),
        name="factor_pass",
    )(gram, kernel_rows, cross_sum)


def local(descriptors, struct_atoms, env_count, sparse_desc, panel_pick):
    n_rows, n_cols = lax.axis_size("rows"), lax.axis_size("cols")
    kernel_rows, gram, cross_sum = gram_pass(
        panel_pick, env_count, struct_atoms, sparse_desc, descriptors, n_rows, n_cols, 512
    )
    factor_rows, kernel_rows, cross_gram = factor_pass(gram, kernel_rows, cross_sum)
    return kernel_rows, factor_rows, cross_gram


def solution(mesh):
    return jax.shard_map(
        local,
        mesh=mesh,
        in_specs=(P("rows", None), P("rows"), P("rows"), P("cols", None), P()),
        out_specs=(P("rows", "cols"), P("rows", None), P("rows", "cols")),
        check_vma=False,
    )
```

```python
import functools

import jax
import jax.numpy as jnp
from jax import lax
from jax.experimental import pallas as pl
from jax.experimental.pallas import tpu as pltpu
from jax.sharding import PartitionSpec as P

MESH = pl.DeviceIdType.MESH
F32 = jnp.float32
BF16 = jnp.bfloat16
TILE = 8
LANES = 128
BAND = 64
MIB = 2**20


def wrap(value, size):
    return jnp.where(value >= size, value - size, value)


def unit_rows(wide):
    mean = jnp.sum(wide * wide, axis=1, keepdims=True) * (1.0 / wide.shape[1])
    return wide * lax.rsqrt(mean + 1e-06)


def each(first, last, body):
    def run(k, carry):
        body(k)
        return carry

    lax.fori_loop(first, last, run, 0)


def gram_kernel(
    n_rows, n_cols, env_total, block,
    pick_ref, count_ref, atoms_ref, sparse_ref, x_ref,
    rows_ref, whole_ref, sum_ref,
    xbuf, kbuf, partial, factor, columns, units, gathered, zbuf, gram, gbuf, lbuf, total_gram, cross, paired, both, cbuf, sumbuf,
    picks, count, xsem, osem, isem, zsend, zrecv, psend, fsend, precv, gsend, csend, wsend, lsend, vsend, rsem,
):
    me = lax.axis_index("rows")
    group = lax.axis_index("cols")
    chip, core = me // 2, lax.rem(me, 2)
    n_chips = n_rows // 2
    slots, depth = xbuf.shape
    width, panel = units.shape[0], gathered.shape[0]
    half, short = depth // 2, width // 2

    def rows_of(i, size):
        return pl.ds(pl.multiple_of(i * size, size), size)

    load_units = pltpu.make_async_copy(sparse_ref, units, isem.at[0])
    load_picks = pltpu.make_async_copy(pick_ref, picks, isem.at[1])
    load_count = pltpu.make_async_copy(count_ref, count, isem.at[2])
    load_units.start()
    load_picks.start()
    load_count.start()
    def load(i):
        at = rows_of(i, block)
        return pltpu.make_async_copy(x_ref.at[at, :], xbuf.at[at, :], xsem.at[i])

    barrier = pltpu.get_barrier_semaphore()
    each(1, n_rows, lambda k: pl.semaphore_signal(
        barrier, inc=1, device_id=(wrap(me + k, n_rows), group), device_id_type=MESH))
    for k in range(1, n_cols):
        pl.semaphore_signal(
            barrier, inc=1, device_id=(me, wrap(group + k, n_cols)), device_id_type=MESH
        )

    load_units.wait()
    load_picks.wait()
    each(0, slots // block, lambda i: load(i).start())

    column = lax.broadcasted_iota(jnp.int32, (16, width), 1) + group * width
    row = lax.broadcasted_iota(jnp.int32, (16, width), 0)
    wanted = jnp.zeros((16, width), jnp.int32)
    for i in range(16):
        wanted = jnp.where(row == i, picks[chip * 16 + i], wanted)
    one_hot = jnp.where(wanted == column, 1.0, 0.0).astype(BF16)
    chosen = unit_rows(jnp.dot(one_hot, units[...], preferred_element_type=F32))
    zbuf[group] = jnp.where(core == 0, chosen[:, :half], chosen[:, half:]).astype(BF16)

    def z_copy(k):
        return pltpu.make_async_remote_copy(
            src_ref=zbuf.at[group], dst_ref=zbuf.at[group],
            send_sem=zsend.at[k - 1], recv_sem=zrecv.at[k - 1],
            device_id=(me, wrap(group + k, n_cols)), device_id_type=MESH,
        )

    pl.semaphore_wait(barrier, n_rows - 1 + n_cols - 1)
    for k in range(1, n_cols):
        z_copy(k).start()

    for i in range(0, width, 128):
        units[i : i + 128, :] = unit_rows(units[i : i + 128, :].astype(F32)).astype(BF16)
    load_count.wait()
    weight = (8.0 * lax.rsqrt(atoms_ref[...].astype(F32))).astype(BF16).astype(F32)
    slot = (
        lax.broadcasted_iota(jnp.int32, atoms_ref.shape, 0) * LANES
        + lax.broadcasted_iota(jnp.int32, atoms_ref.shape, 1)
    )
    roots = jnp.where(slot < count[0], jnp.sqrt(weight * (1.0 / depth)), 0.0).T
    lines = block // LANES
    blocks = slots // block
    for i in range(blocks):
        columns[i] = roots[:, i * lines : (i + 1) * lines]

    def save(i):
        at = rows_of(i, block)
        return pltpu.make_async_copy(
            kbuf.at[at, pl.ds(0, width)], rows_ref.at[at, :], osem.at[i]
        )

    def norms(first, last):
        each(first, last, lambda i: load(i).wait())
        at = slice(first * block, last * block)
        wide = xbuf[at, :].astype(F32)
        mean = jnp.sum(wide * wide, axis=1, keepdims=True) * (1.0 / depth)
        root = jnp.concatenate(
            [columns[i][:, j : j + 1] for i in range(first, last) for j in range(lines)], axis=0
        )
        factor[at, :] = jnp.broadcast_to(
            root * lax.rsqrt(mean + 1e-06), ((last - first) * block, LANES)
        )

    def kernel_of(at, points):
        inner = lax.dot_general(
            xbuf[at, :], points[...], (((1,), (1,)), ((), ())), preferred_element_type=F32
        ) * jnp.concatenate([factor[at, :]] * (points.shape[0] // LANES), axis=1)
        return (inner * inner).astype(BF16)

    def own_points(first, last):
        at = slice(first * block, last * block)
        kbuf[at, :width] = kernel_of(at, units)
        each(first, last, lambda i: save(i).start())

    def panel_half(at, which):
        across = rows_of(which, half)
        return lax.dot_general(
            xbuf[at, across], gathered[:, across], (((1,), (1,)), ((), ())),
            preferred_element_type=F32,
        )

    def panel_points(at):
        inner = partial[at, :] + panel_half(at, 1 - core)
        inner = inner * jnp.concatenate([factor[at, :]] * (panel // LANES), axis=1)
        kbuf[at, width:] = (inner * inner).astype(BF16)

    third = blocks // 3
    late = 2 * third
    norms(0, third)
    own_points(0, third)

    for k in range(1, n_cols):
        z_copy(k).wait()
    total = zbuf[0].astype(F32)
    for k in range(1, n_cols):
        total = total + zbuf[k].astype(F32)

    def piece(which_chip, which_core):
        return gathered.at[rows_of(which_chip, 16), rows_of(which_core, half)]

    piece(chip, core)[...] = total.astype(BF16)

    def plane_copy(k):
        return pltpu.make_async_remote_copy(
            src_ref=piece(chip, core), dst_ref=piece(chip, core),
            send_sem=psend.at[k], recv_sem=precv.at[core, chip],
            device_id=(wrap(chip + k, n_chips) * 2 + core, group), device_id_type=MESH,
        )

    def core_copy(source):
        return pltpu.make_async_remote_copy(
            src_ref=piece(source, core), dst_ref=piece(source, core),
            send_sem=fsend.at[source], recv_sem=precv.at[core, source],
            device_id=(chip * 2 + 1 - core, group), device_id_type=MESH,
        )

    def arrival(source, which_core):
        return pltpu.make_async_copy(
            piece(source, which_core), piece(source, which_core), precv.at[which_core, source]
        )

    each(1, n_chips, lambda k: plane_copy(k).start())
    core_copy(chip).start()
    norms(third, late)
    own_points(third, late)
    norms(late, blocks)
    own_points(late, blocks)

    def forward(k):
        source = wrap(chip + n_chips - k, n_chips)
        arrival(source, core).wait()
        core_copy(source).start()

    each(1, n_chips, forward)

    parts = [slice(i * slots // 3, (i + 1) * slots // 3) for i in range(3)]
    for at in parts:
        partial[at, :] = panel_half(at, core)

    def finish(k):
        source = wrap(chip + n_chips - k, n_chips)
        arrival(source, 1 - core).wait()

    each(0, n_chips, finish)
    for at in parts:
        panel_points(at)

    def transposed_product(right):
        return lax.dot_general(
            kbuf[:, width:], right, (((0,), (0,)), ((), ())), preferred_element_type=F32
        ) * (1.0 / env_total)

    gram[...] = transposed_product(kbuf[:, width:])

    low, high = pl.ds(0, panel // 2), pl.ds(panel // 2, panel // 2)

    def right_copy(k):
        peer = wrap(me + k, n_rows)
        return pltpu.make_async_remote_copy(
            src_ref=gram.at[rows_of(peer, TILE), high], dst_ref=gbuf.at[me],
            send_sem=gsend.at[k], recv_sem=rsem.at[0],
            device_id=(peer, group), device_id_type=MESH,
        )

    def left_copy(k):
        to_chip = wrap(chip + k, n_chips)
        return pltpu.make_async_remote_copy(
            src_ref=gram.at[rows_of(to_chip, TILE), low], dst_ref=lbuf.at[me],
            send_sem=lsend.at[k], recv_sem=rsem.at[3],
            device_id=(to_chip * 2, group), device_id_type=MESH,
        )

    def pair_copy():
        return pltpu.make_async_remote_copy(
            src_ref=cross.at[1 - core], dst_ref=paired,
            send_sem=csend.at[0], recv_sem=rsem.at[5],
            device_id=(chip * 2 + 1 - core, group), device_id_type=MESH,
        )

    def cross_copy(k):
        to_chip = wrap(chip + k, n_chips)
        return pltpu.make_async_remote_copy(
            src_ref=both.at[to_chip], dst_ref=cbuf.at[k - 1],
            send_sem=csend.at[k], recv_sem=rsem.at[1],
            device_id=(to_chip * 2 + core, group), device_id_type=MESH,
        )

    def right_whole(k):
        mine = total_gram.at[rows_of(me, TILE), high]
        return pltpu.make_async_remote_copy(
            src_ref=mine, dst_ref=mine, send_sem=wsend.at[k], recv_sem=rsem.at[2],
            device_id=(wrap(me + k, n_rows), group), device_id_type=MESH,
        )

    def left_whole(k):
        mine = total_gram.at[rows_of(chip, TILE), low]
        return pltpu.make_async_remote_copy(
            src_ref=mine, dst_ref=mine, send_sem=vsend.at[k], recv_sem=rsem.at[4],
            device_id=(wrap(me + k, n_rows), group), device_id_type=MESH,
        )

    def landed(ref, sem):
        pltpu.make_async_copy(ref, ref, sem).wait()

    each(1, n_rows, lambda k: right_copy(k).start())
    each(1, n_chips, lambda k: left_copy(k).start())

    @pl.when(core == 1)
    def _():
        left_copy(0).start()

    total_gram[panel // 2 :, : panel // 2] = jnp.zeros((panel // 2, panel // 2), F32)
    gbuf[me] = gram[rows_of(me, TILE), panel // 2 :]
    lbuf[me] = gram[rows_of(chip, TILE), : panel // 2]
    product = transposed_product(kbuf[:, :width])
    for r in range(panel // TILE):
        part = product[r * TILE : (r + 1) * TILE, :]
        cross[r % 2, r // 2] = jnp.concatenate([part[:, :short], part[:, short:]], axis=0).astype(BF16)
    pair_copy().start()
    pair_copy().wait()
    both[...] = (cross[core].astype(F32) + paired[...].astype(F32)).astype(BF16)
    each(1, n_chips, lambda k: cross_copy(k).start())

    def summed(pieces):
        total = pieces[0]
        for r in range(1, n_rows):
            total = total + pieces[r]
        return total

    others = pl.ds(0, n_rows - 1)
    landed(gbuf.at[others], rsem.at[0])
    total_gram[rows_of(me, TILE), panel // 2 :] = summed(gbuf)
    each(1, n_rows, lambda k: right_whole(k).start())

    @pl.when(core == 0)
    def _():
        landed(lbuf.at[others], rsem.at[3])
        total_gram[rows_of(chip, TILE), : panel // 2] = summed(lbuf)
        each(1, n_rows, lambda k: left_whole(k).start())

    pltpu.make_async_copy(cbuf, cbuf, rsem.at[1]).wait()
    total = both[chip].astype(F32)
    for r in range(n_chips - 1):
        total = total + cbuf[r].astype(F32)
    sumbuf[:, :short] = total[:TILE]
    sumbuf[:, short:] = total[TILE:]
    save_sum = pltpu.make_async_copy(sumbuf, sum_ref, isem.at[3])
    save_sum.start()

    each(1, n_rows, lambda k: right_copy(k).wait_send())
    each(1, n_chips, lambda k: cross_copy(k).wait_send())
    each(1, n_chips, lambda k: left_copy(k).wait_send())
    each(1, n_chips, lambda k: plane_copy(k).wait_send())
    each(0, n_chips, lambda k: core_copy(k).wait_send())
    each(0, blocks, lambda i: save(i).wait())
    landed(total_gram.at[pl.ds(0, panel - TILE), high], rsem.at[2])

    @pl.when(core == 0)
    def _():
        landed(total_gram.at[pl.ds(0, (n_chips - 1) * TILE), low], rsem.at[4])

    @pl.when(core == 1)
    def _():
        landed(total_gram.at[pl.ds(0, n_chips * TILE), low], rsem.at[4])

    save_whole = pltpu.make_async_copy(total_gram, whole_ref, isem.at[4])
    save_whole.start()

    @pl.when(core == 1)
    def _():
        left_copy(0).wait_send()

    @pl.when(core == 0)
    def _():
        each(1, n_rows, lambda k: left_whole(k).wait_send())

    each(1, n_rows, lambda k: right_whole(k).wait_send())
    save_sum.wait()
    save_whole.wait()


def gram_pass(panel_pick, env_count, struct_atoms, sparse_desc, descriptors, n_rows, n_cols, block):
    slots, depth = descriptors.shape
    width, panel = sparse_desc.shape[0], panel_pick.shape[0]
    n_chips = n_rows // 2
    short = width // 2
    hbm = pl.BlockSpec(memory_space=pl.ANY)
    vmem = pl.BlockSpec(memory_space=pltpu.VMEM)
    dma = pltpu.SemaphoreType.DMA
    return pl.pallas_call(
        functools.partial(gram_kernel, n_rows, n_cols, slots // 3 * n_rows, block),
        out_shape=(
            jax.ShapeDtypeStruct((slots, width), BF16),
            jax.ShapeDtypeStruct((panel, panel), F32),
            jax.ShapeDtypeStruct((TILE, width), F32),
        ),
        in_specs=[hbm, hbm, vmem, hbm, hbm],
        out_specs=(hbm, hbm, hbm),
        scratch_shapes=[
            pltpu.VMEM((slots, depth), BF16),
            pltpu.VMEM((slots, width + panel), BF16),
            pltpu.VMEM((slots, panel), F32),
            pltpu.VMEM((slots, LANES), F32),
            pltpu.VMEM((slots // block, LANES, block // LANES), F32),
            pltpu.VMEM((width, depth), BF16),
            pltpu.VMEM((panel, depth), BF16),
            pltpu.VMEM((n_cols, 16, depth // 2), BF16),
            pltpu.VMEM((panel, panel), F32),
            pltpu.VMEM((n_rows, TILE, panel // 2), F32),
            pltpu.VMEM((n_rows, TILE, panel // 2), F32),
            pltpu.VMEM((panel, panel), F32),
            pltpu.VMEM((2, n_chips, 2 * TILE, short), BF16),
            pltpu.VMEM((n_chips, 2 * TILE, short), BF16),
            pltpu.VMEM((n_chips, 2 * TILE, short), BF16),
            pltpu.VMEM((n_chips - 1, 2 * TILE, short), BF16),
            pltpu.VMEM((TILE, width), F32),
            pltpu.SMEM((panel,), jnp.int32),
            pltpu.SMEM((1,), jnp.int32),
            dma((slots // block,)),
            dma((slots // block,)),
            dma((5,)),
            dma((n_cols - 1,)),
            dma((n_cols - 1,)),
            dma((n_chips,)),
            dma((n_chips,)),
            dma((2, n_chips)),
            dma((n_rows,)),
            dma((n_rows,)),
            dma((n_rows,)),
            dma((n_chips,)),
            dma((n_rows,)),
            dma((6,)),
        ],
        compiler_params=pltpu.CompilerParams(
            collective_id=0, has_side_effects=True, vmem_limit_bytes=56 * MIB
        ),
        name="gram_pass",
    )(panel_pick, env_count, struct_atoms.reshape(slots // LANES, LANES), sparse_desc, descriptors)


def wide_of(tile, lane):
    return jnp.broadcast_to(tile[:, lane : lane + 1], (TILE, LANES))


def tall_of(tile, line):
    return jnp.broadcast_to(tile[line : line + 1, :], (TILE, LANES))


def factor_band(tiles, first):
    groups, halves = len(tiles), len(tiles[0])
    line = lax.broadcasted_iota(jnp.int32, (TILE, LANES), 0)
    out = []
    for t in range(groups):
        base = first + t * TILE
        cols = {g: [wide_of(tiles[g][0], base + k) for k in range(TILE)] for g in range(t, groups)}
        low = {(i, k): tall_of(cols[t][k], i) for k in range(TILE) for i in range(k, TILE)}
        inv = []
        for k in range(0, TILE, 2):
            top, mixed, bottom = low[k, k], low[k + 1, k], low[k + 1, k + 1]
            root = lax.rsqrt(top)
            inv.append(root)
            inv.append(top * root * lax.rsqrt(top * bottom - mixed * mixed))
            for i in range(k + 1, TILE):
                low[i, k] = low[i, k] * root
            for i in range(k + 2, TILE):
                low[i, k + 1] = (low[i, k + 1] - low[i, k] * low[k + 1, k]) * inv[k + 1]
            for m in range(k + 2, TILE):
                for i in range(m, TILE):
                    low[i, m] = low[i, m] - (low[i, k] * low[m, k] + low[i, k + 1] * low[m, k + 1])
        band = []
        for h in range(halves):
            lines = []
            for k in range(TILE):
                value = tall_of(tiles[t][h], k)
                for m in range(k):
                    value = value - low[k, m] * lines[m]
                lines.append(value * inv[k])
            band.append(lines)
        merged = []
        for h in range(halves):
            value = band[h][0]
            for k in range(1, TILE):
                value = jnp.where(line == k, band[h][k], value)
            merged.append(value)
        out.append(merged)
        for g in range(t + 1, groups):
            left = []
            for k in range(TILE):
                value = cols[g][k]
                for m in range(k):
                    value = value - left[m] * low[k, m]
                left.append(value * inv[k])
            for h in range(halves):
                terms = [left[k] * band[h][k] for k in range(TILE)]
                while len(terms) > 1:
                    terms = [x + y for x, y in zip(terms[::2], terms[1::2], strict=True)]
                tiles[g][h] = tiles[g][h] - terms[0]
    return out


def factor_kernel(
    gram_ref, rows_ref, sum_ref, out_ref, kernel_ref, cross_ref, work, passing, sums, isem, osem
):
    size = gram_ref.shape[0]
    parts = osem.shape[0] - 1
    part = rows_ref.shape[0] // parts
    chunks = [pl.ds(i * part, part) for i in range(parts)]
    load = pltpu.make_async_copy(gram_ref, work, isem.at[parts])
    loads = [
        pltpu.make_async_copy(rows_ref.at[c, :], passing.at[c, :], isem.at[i])
        for i, c in enumerate(chunks)
    ]
    loads.append(pltpu.make_async_copy(sum_ref, sums, isem.at[parts + 1]))
    saves = [
        pltpu.make_async_copy(passing.at[c, :], kernel_ref.at[c, :], osem.at[i])
        for i, c in enumerate(chunks)
    ]
    saves.append(pltpu.make_async_copy(sums, cross_ref, osem.at[parts]))
    load.start()
    for copy in loads:
        copy.start()
    load.wait()
    halves = size // LANES
    line = lax.broadcasted_iota(jnp.int32, (TILE, LANES), 0)
    lane = lax.broadcasted_iota(jnp.int32, (TILE, LANES), 1)

    def tile(g, h):
        return slice(g * TILE, (g + 1) * TILE), slice(h * LANES, (h + 1) * LANES)

    tall, wide, diagonal = [], [], []
    for h in range(halves):
        along = jnp.zeros((TILE, LANES), F32)
        for g in range(h * LANES // TILE, (h + 1) * LANES // TILE):
            there = jnp.where(lane == line + (g * TILE - h * LANES), work[tile(g, h)], 0.0)
            tall.append(lax.rsqrt(jnp.sum(there, axis=1, keepdims=True)))
            along = along + there
        diagonal.append(jnp.sum(along, axis=0, keepdims=True))
        wide.append(lax.rsqrt(diagonal[h]))
    for g in range(size // TILE):
        for h in range(g * TILE // LANES, halves):
            work[tile(g, h)] = work[tile(g, h)] * tall[g] * wide[h]
    for start in range(0, size, BAND):
        end, near = start + BAND, start // LANES
        tiles = [
            [work[tile(g, h)] for h in range(near, halves)]
            for g in range(start // TILE, end // TILE)
        ]
        factor = factor_band(tiles, start % LANES)
        for i, parts_of in enumerate(factor):
            g = start // TILE + i
            for h in range(halves):
                value = jnp.zeros((TILE, LANES), F32) if h < near else parts_of[h - near]
                if h == near:
                    value = jnp.where(lane >= line + (g * TILE - h * LANES), value, 0.0)
                work[tile(g, h)] = value
        if start == 0:
            for copy, then in zip(loads, saves, strict=True):
                copy.wait()
                then.start()
        if end < size:
            far = end // LANES * LANES
            right = work[start:end, far:]
            inner = lax.dot_general(
                right, right, (((0,), (0,)), ((), ())),
                precision=lax.Precision.HIGHEST, preferred_element_type=F32,
            )
            work[end:, far:] -= inner[end - far :, :]
    me = lax.axis_index("rows")
    out_ref[...] = work[pl.ds(pl.multiple_of(me * TILE, TILE), TILE), :] * jnp.concatenate(
        [diagonal[h] * wide[h] for h in range(halves)], axis=1
    )
    for copy in saves:
        copy.wait()


def factor_pass(gram, kernel_rows, cross_sum):
    size = gram.shape[0]
    hbm = pl.BlockSpec(memory_space=pl.ANY)
    vmem = pl.BlockSpec(memory_space=pltpu.VMEM)
    return pl.pallas_call(
        factor_kernel,
        out_shape=(
            jax.ShapeDtypeStruct((TILE, size), F32),
            jax.ShapeDtypeStruct(kernel_rows.shape, BF16),
            jax.ShapeDtypeStruct(cross_sum.shape, F32),
        ),
        in_specs=[hbm, hbm, hbm],
        out_specs=(vmem, hbm, hbm),
        scratch_shapes=[
            pltpu.VMEM((size, size), F32),
            pltpu.VMEM(kernel_rows.shape, BF16),
            pltpu.VMEM(cross_sum.shape, F32),
            pltpu.SemaphoreType.DMA((8,)),
            pltpu.SemaphoreType.DMA((7,)),
        ],
        compiler_params=pltpu.CompilerParams(vmem_limit_bytes=60 * MIB),
        name="factor_pass",
    )(gram, kernel_rows, cross_sum)


def local(descriptors, struct_atoms, env_count, sparse_desc, panel_pick):
    n_rows, n_cols = lax.axis_size("rows"), lax.axis_size("cols")
    kernel_rows, gram, cross_sum = gram_pass(
        panel_pick, env_count, struct_atoms, sparse_desc, descriptors, n_rows, n_cols, 512
    )
    factor_rows, kernel_rows, cross_gram = factor_pass(gram, kernel_rows, cross_sum)
    return kernel_rows, factor_rows, cross_gram


def solution(mesh):
    return jax.shard_map(
        local,
        mesh=mesh,
        in_specs=(P("rows", None), P("rows"), P("rows"), P("cols", None), P()),
        out_specs=(P("rows", "cols"), P("rows", None), P("rows", "cols")),
        check_vma=False,
    )
```
